32 devices in a mesh: head: 4 (over z), blk: 8 (over y, x, core).
Axes of the slice: x: 2, y: 2, z: 4, core: 2. Of those that a mesh axis runs over, the one named last changes fastest.
Arguments:
- queries: bfloat16 [8, 512, 4096], P('blk', 'head'), may hold values from -6 to 6
- key_rows: bfloat16 [8, 512, 512], P('blk', 'head'), may hold values from -6 to 6
- value_rows: bfloat16 [8, 512, 512], P('blk', 'head'), may hold values from -6 to 6
- attn_out: bfloat16 [8, 512, 4096], P('blk', 'head'), may hold values from -6 to 6
- out_grad: bfloat16 [8, 512, 4096], P('blk', 'head'), may hold values from -3 to 3
- log_norm: float32 [8, 512, 32], P('blk', 'head'), may hold values from 5 to 7
- block_layout: int32 [16], replicated, may hold values from 0 to 15, each once
Outputs:
- query_grad: bfloat16 [8, 512, 4096], P('blk', 'head')
- key_grad: bfloat16 [8, 512, 512], P('blk', 'head')
- value_grad: bfloat16 [8, 512, 512], P('blk', 'head')
The draws below stay inside these ranges and needn't reach their ends.
Inputs may be any that keep to these rules, and one draw needn't show every extreme that they name: Each block number stands once; the rows of blk index b are block block_layout[2 b] followed by block block_layout[2 b + 1].
All inputs are finite; a program needn't handle non-finite values.
Results may differ from the reference program's by a relative error of at most 0.014.
Values may be sent and summed in bfloat16 or wider, within the bound.
No kernel may reach another device: no remote copies, remote signals or barrier semaphores. Data moves between devices by JAX's collectives and lax.ppermute only.
A program may use at most 128 MiB of HBM per device.

```python
import math
import jax
import jax.numpy as jnp
from jax import lax

HD = 128
KV_HEADS = 4
GROUP = 8
STEPS = 4
QH = 32
ROWS = 512
BLOCK = 256
BLOCKS = 16
N_BLK = 8


def levels(stream_key, extent, split, low, largest):
    loudness, own = 1.0, jax.random.fold_in(stream_key, 6)
    for dim, parts in split:
        heights = jnp.exp(jax.random.uniform(jax.random.fold_in(own, dim), (parts,), jnp.float32, low / len(split), largest / len(split)))
        loudness = loudness * jnp.repeat(heights, extent[dim] // parts).reshape([-1 if axis == dim else 1 for axis in range(len(extent))])
    return loudness


def bell_draw(rng, shape, scale, limit, split=(), kind=jnp.bfloat16):
    entries = scale * jax.random.normal(rng, shape, jnp.float32)
    if split:
        entries = entries * levels(rng, shape, split, -0.22, 0.18)
    return jnp.clip(entries, -limit, limit).astype(kind)


def setup_inputs(seed: int = 0) -> dict:
    seeds = jax.random.split(jax.random.key(seed), 8)
    queries = bell_draw(seeds[0], (N_BLK, ROWS, QH * HD), 1.0, 6.0, ((0, 8), (1, 4)))
    key_rows = bell_draw(seeds[1], (N_BLK, ROWS, KV_HEADS * HD), 1.0, 6.0, ((0, 8), (1, 4)))
    value_rows = bell_draw(seeds[2], (N_BLK, ROWS, KV_HEADS * HD), 1.0, 6.0, ((0, 8), (1, 4)))
    attn_out = bell_draw(seeds[3], (N_BLK, ROWS, QH * HD), 1.0, 6.0, ((0, 8), (1, 4)))
    out_grad = bell_draw(seeds[4], (N_BLK, ROWS, QH * HD), 0.5, 3.0, ((0, 8), (1, 4)))
    log_norm = jnp.clip(5.0 + 2.0 * jax.random.uniform(seeds[5], (N_BLK, ROWS, QH), jnp.float32) ** levels(seeds[5], (N_BLK, ROWS, QH), ((0, 8), (1, 4)), -0.2, 0.2), 5.0, 7.0)
    block_layout = jax.random.permutation(seeds[6], BLOCKS).astype(jnp.int32)
    return dict(queries=queries, key_rows=key_rows, value_rows=value_rows, attn_out=attn_out, out_grad=out_grad, log_norm=log_norm, block_layout=block_layout)


def tile_terms(query, dout, lse, delta, keys, vals, qpos, kpos, scale):
    f32 = jnp.float32
    scores = jnp.einsum('rkgd,ckd->kgrc', query.astype(f32), keys.astype(f32)) * scale
    linked = qpos[:, None] >= kpos[None, :]
    lse_t = jnp.transpose(lse, (1, 2, 0))
    delta_t = jnp.transpose(delta, (1, 2, 0))
    prob = jnp.where(linked[None, None], jnp.exp(scores - lse_t[..., None]), 0.0)
    prob16 = prob.astype(jnp.bfloat16)
    dprob = jnp.einsum('rkgd,ckd->kgrc', dout.astype(f32), vals.astype(f32))
    dscore = (prob * (dprob - delta_t[..., None])).astype(jnp.bfloat16)
    dval = jnp.einsum('kgrc,rkgd->ckd', prob16.astype(f32), dout.astype(f32))
    dkey = jnp.einsum('kgrc,rkgd->ckd', dscore.astype(f32), query.astype(f32))
    dquery = jnp.einsum('kgrc,ckd->rkgd', dscore.astype(f32), keys.astype(f32))
    return (dquery, dkey, dval)

def reference(queries, key_rows, value_rows, attn_out, out_grad, log_norm, block_layout):
    nblk, rows = (queries.shape[0], queries.shape[1])
    scale = 1.0 / math.sqrt(HD)
    qall = queries.reshape(nblk, rows, KV_HEADS, GROUP, HD)
    dall = out_grad.reshape(nblk, rows, KV_HEADS, GROUP, HD)
    oall = attn_out.reshape(nblk, rows, KV_HEADS, GROUP, HD)
    kall = key_rows.reshape(nblk, rows, KV_HEADS, HD)
    vall = value_rows.reshape(nblk, rows, KV_HEADS, HD)
    lall = log_norm.reshape(nblk, rows, KV_HEADS, GROUP)
    offsets = jnp.arange(rows, dtype=jnp.int32)
    within = offsets % BLOCK
    second = offsets // BLOCK

    def positions(owner):
        return jnp.take(block_layout, 2 * owner + second) * BLOCK + within

    def one_group(carry, index):
        dk_all, dv_all = carry
        query = qall[index]
        dout = dall[index]
        delta = lax.optimization_barrier(jnp.sum(dout.astype(jnp.float32) * oall[index].astype(jnp.float32), axis=-1))
        qpos = positions(index)
        dq_acc = jnp.zeros((rows, KV_HEADS, GROUP, HD), jnp.float32)
        for step in range(STEPS):
            owner = (index - step) % nblk
            dquery, dkey, dval = tile_terms(query, dout, lall[index], delta, kall[owner], vall[owner], qpos, positions(owner), scale)
            dq_acc = dq_acc + dquery
            dk_all = dk_all.at[owner].add(dkey)
            dv_all = dv_all.at[owner].add(dval)
        return ((dk_all, dv_all), dq_acc)
    start = (jnp.zeros((nblk, rows, KV_HEADS, HD), jnp.float32), jnp.zeros((nblk, rows, KV_HEADS, HD), jnp.float32))
    (dk_all, dv_all), dq_all = lax.scan(one_group, start, jnp.arange(nblk, dtype=jnp.int32))
    query_grad = (dq_all * scale).astype(jnp.bfloat16).reshape(nblk, rows, KV_HEADS * GROUP * HD)
    key_grad = (dk_all * scale).astype(jnp.bfloat16).reshape(nblk, rows, KV_HEADS * HD)
    value_grad = dv_all.astype(jnp.bfloat16).reshape(nblk, rows, KV_HEADS * HD)
    return (query_grad, key_grad, value_grad)
```

```python
import functools
import math

import jax
import jax.numpy as jnp
from jax import lax
from jax.experimental import pallas as pl
from jax.experimental.pallas import tpu as pltpu
from jax.sharding import PartitionSpec as P

HD = 128
GROUP = 8
QUAD = 4
SCALE = 1.0 / math.sqrt(HD)
LOG2E = math.log2(math.e)
FAR = 1e30
TERM_ROWS = 16
COVER = 12
F32 = jnp.float32
BF16 = jnp.bfloat16
SMEM = pl.BlockSpec(memory_space=pltpu.SMEM)
VMEM = pl.BlockSpec(memory_space=pltpu.VMEM)
ANY = pl.BlockSpec(memory_space=pl.ANY)


def shifted(block, axis, distance):
    size = lax.axis_size(axis)
    route = [((i - distance) % size, i) for i in range(size)]
    return lax.ppermute(block, axis, route)


def crossed(block, mask):
    return lax.ppermute(block, "blk", [(i, i ^ mask) for i in range(lax.axis_size("blk"))])


def hopped(block, mask):
    n_z, n_blk = lax.axis_size("head"), lax.axis_size("blk")
    route = [(i * n_blk + b, (i + 1) % n_z * n_blk + (b ^ mask)) for i in range(n_z) for b in range(n_blk)]
    return lax.ppermute(block, ("head", "blk"), route)


def member(meta, mask):
    c = meta[0] % QUAD
    if mask & 1:
        c = c + 1 - 2 * (c % 2)
    if mask & 2:
        c = (c + 2) % QUAD
    return c


def block_of(meta, mask, size):
    return pl.ds(pl.multiple_of(member(meta, mask) * size, size), size)


def pack_kv(meta, keys, vals, *outs):
    for mask, out in enumerate(outs):
        cols = block_of(meta, mask, HD)
        out[0], out[1] = keys[0, :, cols], vals[0, :, cols]


def join_kv(meta, *refs):
    parts, (ring, tail) = refs[:QUAD], refs[QUAD:]
    tok = parts[0].shape[1]
    for mask, part in enumerate(parts):
        ring[:, block_of(meta, mask, tok), :] = part[...]
    tail[...] = ring[:, tok:, :]


def pack_rows(meta, queries, douts, outs, lse, _, *refs):
    packed, lse_t = refs[:QUAD], refs[QUAD]
    tok = queries.shape[1]
    wide = GROUP * HD
    lse_t[...] = lse[0].T * LOG2E
    for mask, out in enumerate(packed):
        cols = block_of(meta, mask, wide)
        out[0:tok, :] = queries[0, :, cols]
        out[tok:2 * tok, :] = douts[0, :, cols]
        norms = lse_t[block_of(meta, mask, GROUP), :]
        for h in range(GROUP):
            at = slice(h * HD, (h + 1) * HD)
            head = pl.ds(pl.multiple_of(member(meta, mask) * wide + h * HD, HD), HD)
            prod = out[tok:2 * tok, at].astype(F32) * outs[0, :, head].astype(F32)
            delta = jnp.sum(prod.T, axis=0, keepdims=True)
            lines = []
            for term in (norms[h:h + 1], delta):
                high = term.astype(BF16).astype(F32)
                lines += [high, term - high]
            block = jnp.concatenate(lines + [jnp.zeros((TERM_ROWS - 4, tok), F32)], axis=0).astype(BF16)
            out[2 * tok:, h * tok:(h + 1) * tok] = block


def do_nothing(*refs):
    del refs


def later(block, after):
    return pl.pallas_call(
        do_nothing,
        out_shape=jax.ShapeDtypeStruct(block.shape, block.dtype),
        in_specs=[ANY] * (1 + len(after)),
        out_specs=ANY,
        input_output_aliases={0: 0},
        compiler_params=pltpu.CompilerParams(vmem_limit_bytes=2**20),
        name="later",
    )(block, *after)


def pass_on(ring_in, *refs):
    tail = refs[-1]
    tail[...] = ring_in[:, ring_in.shape[1] - tail.shape[1]:, :]


def held(ring, after):
    planes, rows, cols = ring.shape
    return pl.pallas_call(
        pass_on,
        out_shape=[
            jax.ShapeDtypeStruct(ring.shape, ring.dtype),
            jax.ShapeDtypeStruct((planes, rows // QUAD * (QUAD - 1), cols), ring.dtype),
        ],
        in_specs=[VMEM] + [ANY] * len(after),
        out_specs=[ANY, VMEM],
        input_output_aliases={0: 0},
        compiler_params=pltpu.CompilerParams(vmem_limit_bytes=4 * 2**20),
        name="pass_on",
    )(ring, *after)


def total(n_packet, d_own, back, refs):
    tok = d_own.shape[1] // QUAD
    tail = d_own[:, tok:, :] + back[...].astype(F32)
    lead = d_own[:, 0:tok, :]
    if n_packet:
        lead += refs[0][:, 0:tok, :].astype(F32)
        tail += refs[0][:, tok:, :].astype(F32)
    return lead, tail


def pack_sum(n_packet, d_own, back, *refs):
    lead, tail = total(n_packet, d_own, back, refs)
    out = refs[-1]
    tok = lead.shape[1]
    out[:, 0:tok, :] = lead.astype(BF16)
    out[:, tok:, :] = tail.astype(BF16)


def split_sum(meta, d_own, back, packet, *refs):
    outs, whole = refs[:QUAD], refs[QUAD]
    lead, tail = total(1, d_own, back, (packet,))
    tok = lead.shape[1]
    whole[:, 0:tok, :] = lead
    whole[:, tok:, :] = tail
    for mask, out in enumerate(outs):
        out[...] = whole[:, block_of(meta, mask, tok), :].astype(BF16)


def pack_cross(masks, meta, *refs):
    n = len(masks)
    dqs, (d_own, back), outs, whole = refs[:n], refs[n:n + 2], refs[n + 2:-1], refs[-1]
    lead, tail = total(0, d_own, back, ())
    tok, wide = dqs[0].shape
    whole[:, 0:tok, :] = lead
    whole[:, tok:, :] = tail
    for mask, dq, out in zip(masks, dqs, outs):
        out[:, 0:wide] = dq[...]
        part = whole[:, block_of(meta, mask, tok), :].astype(BF16)
        out[:, wide:wide + HD] = part[0]
        out[:, wide + HD:] = part[1]
    if len(outs) > n:
        outs[n][...] = whole[:, block_of(meta, 0, tok), :]


def place_heads(meta, dq_own, got_one, got_two, got_three, out, done, sems):
    wide = dq_own.shape[1]
    copies = []
    for mask, src in enumerate((dq_own, got_one, got_two, got_three)):
        src = src if mask == 0 else src.at[:, 0:wide]
        copies.append(pltpu.make_async_copy(src, out.at[0, :, block_of(meta, mask, wide)], sems.at[mask]))
    for copy in copies:
        copy.start()
    done[...] = jnp.zeros_like(done)
    for copy in copies:
        copy.wait()


def finish(meta, kept, got_one, got_two, got_three, hop0, hop1, hop2, hop3, _, dkey, dval):
    wide = got_one.shape[1] - 2 * HD
    for mask, (got, hop) in enumerate(zip((kept, got_one, got_two, got_three), (hop0, hop1, hop2, hop3))):
        cols = block_of(meta, mask, HD)
        for plane, dst in ((0, dkey), (1, dval)):
            first = got[plane] if mask == 0 else got[:, wide + plane * HD:wide + (plane + 1) * HD].astype(F32)
            dst[0, :, cols] = (first + hop[plane].astype(F32)).astype(BF16)


def small_call(body, outs, specs, operands, scratch=(), cost=0, far_out=False):
    shapes = [jax.ShapeDtypeStruct(shape, kind) for shape, kind in outs]
    name = getattr(body, "func", body).__name__
    return pl.pallas_call(
        body,
        out_shape=shapes,
        in_specs=specs,
        out_specs=[ANY if i == 0 and far_out else VMEM for i in range(len(shapes))],
        scratch_shapes=list(scratch),
        compiler_params=pltpu.CompilerParams(vmem_limit_bytes=4 * 2**20),
        cost_estimate=pl.CostEstimate(flops=0, bytes_accessed=cost, transcendentals=0),
        name=name,
    )(*operands)


def attend(lag, masks, n_blk, n_z, first, last, closing, n_after, meta, layout, *refs):
    (rows_a, rows_b, near, far), refs = refs[:4], refs[4:]
    tok = near.shape[1] // QUAD
    if not first:
        acc_in, refs = refs[0], refs[1:]
    if closing:
        d_in, refs = refs[0], refs[1:]
    refs = refs[n_after:]
    if last:
        dq_outs, refs = refs[:2], refs[2:]
    else:
        acc_out, refs = refs[0], refs[1:]
    if closing:
        (d_own, d_far), refs = refs[:2], refs[2:]
    else:
        d_out, refs = refs[0], refs[1:]
    kbuf, vbuf, kbuf_t, dbuf, probs, dscores = refs
    n_far = QUAD - 1
    window = QUAD * tok
    quad = meta[0] - meta[0] % QUAD
    z = meta[1]
    shard = (z + n_z - lag) % n_z

    for plane, dst in ((0, kbuf), (1, vbuf)):
        dst[0:n_far * tok, :] = far[plane]
        dst[n_far * tok:, :] = near[plane]
    kbuf_t[...] = kbuf[...].T
    dbuf[...] = d_in[...] if closing else jnp.zeros_like(dbuf)

    def base(group, shard):
        return layout[2 * group + shard // 2] * (2 * tok) + (shard % 2) * tok

    for t, (mask, rows) in enumerate(zip(masks, (rows_a, rows_b))):
        i = member(meta, mask)
        chunk = pl.ds(pl.multiple_of(i * tok, tok), window)
        keys, vals, keys_t = kbuf[chunk, :], vbuf[chunk, :], kbuf_t[:, chunk]
        qbase = base(quad + i, z)
        gaps = [qbase - base((quad + i - n_far + c + n_blk) % n_blk, shard) for c in range(QUAD)]
        row = lax.broadcasted_iota(jnp.int32, (tok, 2 * tok), 0)
        col = lax.broadcasted_iota(jnp.int32, (tok, 2 * tok), 1) % tok
        linked = (col - row + gaps[QUAD - 1]) >= 0

        def stacked(start, heads):
            return jnp.concatenate([rows[start:start + tok, h * HD:(h + 1) * HD] for h in heads], axis=0)

        for g in range(GROUP // 2):
            heads = (2 * g, 2 * g + 1)
            query, dout = stacked(0, heads), stacked(tok, heads)
            span = slice(2 * g * tok, (2 * g + 2) * tok)
            terms = rows[2 * tok:, span].astype(F32)
            lse, delta = terms[0:1] + terms[1:2], terms[2:3] + terms[3:4]
            nt = (((1,), (1,)), ((), ()))
            score = lax.dot_general(keys, query, nt, preferred_element_type=F32) * (SCALE * LOG2E)
            dprob = lax.dot_general(vals, dout, nt, preferred_element_type=F32)
            for c in range(QUAD):
                part = slice(c * tok, (c + 1) * tok)
                if c == QUAD - 1:
                    prob = jnp.where(linked, jnp.exp2(score[part] - lse), 0.0)
                else:
                    prob = jnp.exp2(score[part] - jnp.where(gaps[c] > 0, lse, FAR))
                probs[t, part, span] = prob.astype(BF16)
                dscores[t, part, span] = (prob * (dprob[part] - delta)).astype(BF16)
        query, dout = stacked(0, range(GROUP)), stacked(tok, range(GROUP))
        dbuf[0, chunk, :] += jnp.dot(dscores[t], query, preferred_element_type=F32)
        dbuf[1, chunk, :] += jnp.dot(probs[t], dout, preferred_element_type=F32)
        dq = jnp.dot(keys_t, dscores[t], preferred_element_type=F32)
        if not first:
            dq = dq + acc_in[t]
        if last:
            for h in range(GROUP):
                at = slice(h * HD, (h + 1) * HD)
                dq_outs[t][:, at] = (dq[:, h * tok:(h + 1) * tok] * SCALE).T.astype(BF16)
        else:
            acc_out[t] = dq

    if closing:
        for plane, scale in ((0, SCALE), (1, 1.0)):
            d_far[plane] = (dbuf[plane, 0:n_far * tok, :] * scale).astype(BF16)
            d_own[plane] = dbuf[plane, n_far * tok:, :] * scale
    else:
        d_out[...] = dbuf[...]


def attend_call(lag, masks, n_blk, n_z, meta, layout, rows, keys, acc, d_in, after):
    tok = keys[0].shape[1] // QUAD
    first, last, closing = acc is None, lag == n_z - 1, d_in is not None
    chunks = (2 * QUAD - 1) * tok
    near, far = (2, QUAD * tok, HD), (2, (QUAD - 1) * tok, HD)
    outs = (
        [jax.ShapeDtypeStruct((tok, GROUP * HD), BF16)] * 2
        if last else [jax.ShapeDtypeStruct((2, HD, GROUP * tok), F32)]
    )
    n_heads = len(outs)
    if closing:
        outs = outs + [jax.ShapeDtypeStruct(near, F32), jax.ShapeDtypeStruct(far, BF16)]
    else:
        outs = outs + [jax.ShapeDtypeStruct((2, chunks, HD), F32)]
    inputs = [meta, layout, *rows, *keys]
    aliases = {}
    if not first:
        if not last:
            aliases[len(inputs)] = 0
        inputs.append(acc)
    if closing:
        inputs.append(d_in)
    results = pl.pallas_call(
        functools.partial(attend, lag, masks, n_blk, n_z, first, last, closing, len(after)),
        out_shape=outs,
        in_specs=[SMEM, SMEM] + [VMEM] * (len(inputs) - 2) + [ANY] * len(after),
        out_specs=[VMEM] * len(outs),
        scratch_shapes=[
            pltpu.VMEM((chunks, HD), BF16),
            pltpu.VMEM((chunks, HD), BF16),
            pltpu.VMEM((HD, chunks), BF16),
            pltpu.VMEM((2, chunks, HD), F32),
            pltpu.VMEM((2, QUAD * tok, GROUP * tok), BF16),
            pltpu.VMEM((2, QUAD * tok, GROUP * tok), BF16),
        ],
        input_output_aliases=aliases,
        compiler_params=pltpu.CompilerParams(vmem_limit_bytes=14 * 2**20),
        cost_estimate=pl.CostEstimate(
            flops=COVER * 4 * tok * GROUP * tok * HD, bytes_accessed=2**20, transcendentals=0
        ),
        name="attend",
    )(*inputs, *after)
    return results[:n_heads], results[n_heads:]


def shards(queries, key_rows, value_rows, attn_out, out_grad, log_norm, block_layout):
    tok = queries.shape[1]
    blk, z = lax.axis_index("blk"), lax.axis_index("head")
    n_blk, n_z = lax.axis_size("blk"), lax.axis_size("head")
    wide = GROUP * HD
    meta = jnp.stack([blk, z]).astype(jnp.int32)
    piece = ((2, tok, HD), BF16)
    ring_of, tail_of = ((2, QUAD * tok, HD), BF16), ((2, (QUAD - 1) * tok, HD), BF16)

    pieces = small_call(pack_kv, [piece] * QUAD, [SMEM, VMEM, VMEM], [meta, key_rows, value_rows])
    parts = [pieces[0]] + [crossed(pieces[mask], mask) for mask in range(1, QUAD)]
    ring, tail = small_call(join_kv, [ring_of, tail_of], [SMEM] + [VMEM] * QUAD, [meta, *parts])
    block = ((2 * tok + TERM_ROWS, wide), BF16)
    packed = small_call(
        pack_rows, [block] * QUAD, [SMEM] + [VMEM] * 4 + [ANY],
        [meta, queries, out_grad, attn_out, log_norm, pieces[0]],
        scratch=[pltpu.VMEM((log_norm.shape[2], tok), F32)], cost=4 * 2**20,
    )
    rows = [packed[0]] + [crossed(later(packed[mask], [tail]), mask) for mask in range(1, QUAD)]

    keys = [[ring, shifted(tail, "blk", QUAD)]]
    accs = [None, None]
    sums, backs = [None] * n_z, [None] * n_z

    def pass_keys(after):
        ring, tail = held(shifted(keys[-1][0], "head", 1), after)
        keys.append([ring, shifted(tail, "blk", QUAD)])

    def call(pair, lag, after=()):
        heads, grads = attend_call(
            lag, (2 * pair, 2 * pair + 1), n_blk, n_z, meta, block_layout, rows[2 * pair:2 * pair + 2], keys[lag],
            accs[pair], sums[lag], after,
        )
        accs[pair] = heads if lag == n_z - 1 else heads[0]
        if sums[lag] is not None:
            backs[lag] = shifted(grads[1], "blk", -QUAD)
        sums[lag] = grads[0]

    def pass_sums(lag, packet, after):
        parts = [sums[lag], backs[lag], *packet]
        out = small_call(
            functools.partial(pack_sum, len(packet)), [ring_of], [VMEM] * len(parts) + [ANY], parts + [after]
        )[0]
        return [shifted(out, "head", 1)]

    call(0, 0)
    pass_keys([accs[0]])
    call(0, 1)
    pass_keys([accs[0]])
    call(0, 2)
    pass_keys([accs[0]])
    call(1, 0, [accs[0]])
    call(1, 1)
    call(1, 2, [backs[0]])
    packet = pass_sums(1, [], accs[1])
    call(1, 3)
    cross = ((tok, wide + 2 * HD), BF16)
    whole = pltpu.VMEM(ring_of[0], F32)
    sent = small_call(
        functools.partial(pack_cross, (2, 3)), [cross] * 2, [SMEM] + [VMEM] * 4,
        [meta, *accs[1], sums[0], backs[0]], scratch=[whole], cost=2**20,
    )
    call(0, 3, [accs[1][0]])
    packet = pass_sums(2, packet, sums[3])
    near_sent, kept = small_call(
        functools.partial(pack_cross, (1,)), [cross, (piece[0], F32)], [SMEM] + [VMEM] * 3,
        [meta, accs[0][1], sums[0], backs[0]], scratch=[whole], cost=2**20,
    )
    got = [crossed(part, mask) for mask, part in enumerate([near_sent, *sent], 1)]
    hops = small_call(
        split_sum, [piece] * QUAD, [SMEM] + [VMEM] * 3, [meta, sums[3], backs[3], *packet],
        scratch=[pltpu.VMEM(ring_of[0], F32)],
    )
    hops = [hopped(hops[mask], mask) for mask in range(QUAD)]
    query_grad, placed = small_call(
        place_heads, [(queries.shape, BF16), ((8, HD), F32)], [SMEM] + [VMEM] * QUAD, [meta, accs[0][0], *got],
        scratch=[pltpu.SemaphoreType.DMA((QUAD,))], far_out=True,
    )
    flat = (key_rows.shape, BF16)
    key_grad, value_grad = small_call(
        finish, [flat, flat], [SMEM] + [VMEM] * 8 + [ANY], [meta, kept, *got, *hops, placed]
    )
    return query_grad, key_grad, value_grad


def solution(mesh):
    spread = P("blk", "head", None)
    return jax.shard_map(
        shards,
        mesh=mesh,
        in_specs=(spread,) * 6 + (P(),),
        out_specs=(spread,) * 3,
        check_vma=False,
    )
```

```python
import functools
import math

import jax
import jax.numpy as jnp
from jax import lax
from jax.experimental import pallas as pl
from jax.experimental.pallas import tpu as pltpu
from jax.sharding import PartitionSpec as P

HD = 128
GROUP = 8
QUAD = 4
SCALE = 1.0 / math.sqrt(HD)
LOG2E = math.log2(math.e)
FAR = 1e30
TERM_ROWS = 16
COVER = 12
F32 = jnp.float32
BF16 = jnp.bfloat16
SMEM = pl.BlockSpec(memory_space=pltpu.SMEM)
VMEM = pl.BlockSpec(memory_space=pltpu.VMEM)
ANY = pl.BlockSpec(memory_space=pl.ANY)


def shifted(block, axis, distance):
    size = lax.axis_size(axis)
    route = [((i - distance) % size, i) for i in range(size)]
    return lax.ppermute(block, axis, route)


def crossed(block, mask):
    return lax.ppermute(block, "blk", [(i, i ^ mask) for i in range(lax.axis_size("blk"))])


def hopped(block, mask):
    n_z, n_blk = lax.axis_size("head"), lax.axis_size("blk")
    route = [(i * n_blk + b, (i + 1) % n_z * n_blk + (b ^ mask)) for i in range(n_z) for b in range(n_blk)]
    return lax.ppermute(block, ("head", "blk"), route)


def member(meta, mask):
    c = meta[0] % QUAD
    if mask & 1:
        c = c + 1 - 2 * (c % 2)
    if mask & 2:
        c = (c + 2) % QUAD
    return c


def block_of(meta, mask, size):
    return pl.ds(pl.multiple_of(member(meta, mask) * size, size), size)


def pack_kv(meta, keys, vals, *outs):
    for mask, out in enumerate(outs):
        cols = block_of(meta, mask, HD)
        out[0], out[1] = keys[0, :, cols], vals[0, :, cols]


def join_kv(meta, *refs):
    parts, (ring, tail) = refs[:QUAD], refs[QUAD:]
    tok = parts[0].shape[1]
    for mask, part in enumerate(parts):
        ring[:, block_of(meta, mask, tok), :] = part[...]
    tail[...] = ring[:, tok:, :]


def pack_rows(meta, queries, douts, outs, lse, _, *refs):
    packed, lse_t = refs[:QUAD], refs[QUAD]
    tok = queries.shape[1]
    wide = GROUP * HD
    lse_t[...] = lse[0].T * LOG2E
    for mask, out in enumerate(packed):
        cols = block_of(meta, mask, wide)
        out[0:tok, :] = queries[0, :, cols]
        out[tok:2 * tok, :] = douts[0, :, cols]
        norms = lse_t[block_of(meta, mask, GROUP), :]
        for h in range(GROUP):
            at = slice(h * HD, (h + 1) * HD)
            head = pl.ds(pl.multiple_of(member(meta, mask) * wide + h * HD, HD), HD)
            prod = out[tok:2 * tok, at].astype(F32) * outs[0, :, head].astype(F32)
            delta = jnp.sum(prod.T, axis=0, keepdims=True)
            lines = []
            for term in (norms[h:h + 1], delta):
                high = term.astype(BF16).astype(F32)
                lines += [high, term - high]
            block = jnp.concatenate(lines + [jnp.zeros((TERM_ROWS - 4, tok), F32)], axis=0).astype(BF16)
            out[2 * tok:, h * tok:(h + 1) * tok] = block


def do_nothing(*refs):
    del refs


def later(block, after=(), cost=0):
    return pl.pallas_call(
        do_nothing,
        out_shape=jax.ShapeDtypeStruct(block.shape, block.dtype),
        in_specs=[ANY] * (1 + len(after)),
        out_specs=ANY,
        input_output_aliases={0: 0},
        compiler_params=pltpu.CompilerParams(vmem_limit_bytes=2**20),
        cost_estimate=pl.CostEstimate(flops=cost, bytes_accessed=0, transcendentals=0),
        name="later",
    )(block, *after)


def pass_on(ring_in, *refs):
    tail = refs[-1]
    tail[...] = ring_in[:, ring_in.shape[1] - tail.shape[1]:, :]


def held(ring, after):
    planes, rows, cols = ring.shape
    return pl.pallas_call(
        pass_on,
        out_shape=[
            jax.ShapeDtypeStruct(ring.shape, ring.dtype),
            jax.ShapeDtypeStruct((planes, rows // QUAD * (QUAD - 1), cols), ring.dtype),
        ],
        in_specs=[VMEM] + [ANY] * len(after),
        out_specs=[ANY, VMEM],
        input_output_aliases={0: 0},
        compiler_params=pltpu.CompilerParams(vmem_limit_bytes=4 * 2**20),
        name="pass_on",
    )(ring, *after)


def total(part, n_packet, d_own, back, refs):
    tok = d_own.shape[1] // QUAD
    tail = d_own[:, tok:, :] + back[2 * part:2 * part + 2].astype(F32)
    lead = d_own[:, 0:tok, :]
    if n_packet:
        lead += refs[0][:, 0:tok, :].astype(F32)
        tail += refs[0][:, tok:, :].astype(F32)
    return lead, tail


def pack_sum(part, n_packet, d_own, back, *refs):
    lead, tail = total(part, n_packet, d_own, back, refs)
    out = refs[-1]
    tok = lead.shape[1]
    out[:, 0:tok, :] = lead.astype(BF16)
    out[:, tok:, :] = tail.astype(BF16)


def split_sum(meta, d_own, back, packet, *refs):
    outs, whole = refs[:QUAD], refs[QUAD]
    lead, tail = total(0, 1, d_own, back, (packet,))
    tok = lead.shape[1]
    whole[:, 0:tok, :] = lead
    whole[:, tok:, :] = tail
    for mask, out in enumerate(outs):
        out[...] = whole[:, block_of(meta, mask, tok), :].astype(BF16)


def pack_cross(masks, meta, *refs):
    n = len(masks)
    dqs, (d_own, back), outs, whole = refs[:n], refs[n:n + 2], refs[n + 2:-1], refs[-1]
    lead, tail = total(0, 0, d_own, back, ())
    tok, wide = dqs[0].shape
    whole[:, 0:tok, :] = lead
    whole[:, tok:, :] = tail
    for mask, dq, out in zip(masks, dqs, outs):
        out[:, 0:wide] = dq[...]
        part = whole[:, block_of(meta, mask, tok), :].astype(BF16)
        out[:, wide:wide + HD] = part[0]
        out[:, wide + HD:] = part[1]


def pack_near(meta, dq, d_own, back, _, first, second, kept, whole):
    lead, tail = total(0, 0, d_own, back, ())
    tok, wide = dq.shape
    half = first.shape[1]
    whole[:, 0:tok, :] = lead
    whole[:, tok:, :] = tail
    part = whole[:, block_of(meta, 1, tok), :].astype(BF16)
    first[...] = dq[:, 0:half]
    second[:, 0:wide - half] = dq[:, half:]
    second[:, wide - half:wide - half + HD] = part[0]
    second[:, wide - half + HD:] = part[1]
    kept[...] = whole[:, block_of(meta, 0, tok), :]


def place_heads(meta, dq_own, near_one, near_two, got_two, got_three, out, done, sems):
    wide = dq_own.shape[1]
    half = near_one.shape[1]
    copies = []
    for mask, src in ((0, dq_own), (2, got_two.at[:, 0:wide]), (3, got_three.at[:, 0:wide])):
        copies.append(pltpu.make_async_copy(src, out.at[0, :, block_of(meta, mask, wide)], sems.at[len(copies)]))
    for start, src in ((0, near_one), (half, near_two.at[:, 0:wide - half])):
        cols = pl.ds(pl.multiple_of(member(meta, 1) * wide + start, HD), src.shape[1])
        copies.append(pltpu.make_async_copy(src, out.at[0, :, cols], sems.at[len(copies)]))
    for copy in copies:
        copy.start()
    done[...] = jnp.zeros_like(done)
    for copy in copies:
        copy.wait()


def finish(meta, kept, near_two, got_two, got_three, hop0, hop1, hop2, hop3, _, dkey, dval):
    for mask, (got, hop) in enumerate(zip((kept, near_two, got_two, got_three), (hop0, hop1, hop2, hop3))):
        cols = block_of(meta, mask, HD)
        for plane, dst in ((0, dkey), (1, dval)):
            if mask == 0:
                first = got[plane]
            else:
                start = got.shape[1] - (2 - plane) * HD
                first = got[:, start:start + HD].astype(F32)
            dst[0, :, cols] = (first + hop[plane].astype(F32)).astype(BF16)


def small_call(body, outs, specs, operands, scratch=(), cost=0, far_out=False):
    shapes = [jax.ShapeDtypeStruct(shape, kind) for shape, kind in outs]
    name = getattr(body, "func", body).__name__
    return pl.pallas_call(
        body,
        out_shape=shapes,
        in_specs=specs,
        out_specs=[ANY if i == 0 and far_out else VMEM for i in range(len(shapes))],
        scratch_shapes=list(scratch),
        compiler_params=pltpu.CompilerParams(vmem_limit_bytes=4 * 2**20),
        cost_estimate=pl.CostEstimate(flops=0, bytes_accessed=cost, transcendentals=0),
        name=name,
    )(*operands)


def attend(lag, masks, n_blk, n_z, first, last, closing, n_after, place, meta, layout, *refs):
    (rows_a, rows_b, near, far), refs = refs[:4], refs[4:]
    tok = near.shape[1] // QUAD
    if not first:
        acc_in, refs = refs[0], refs[1:]
    if closing:
        d_in, refs = refs[0], refs[1:]
    refs = refs[n_after:]
    if last:
        dq_outs, refs = refs[:2], refs[2:]
    else:
        acc_out, refs = refs[0], refs[1:]
    if closing:
        (d_own, d_far), refs = refs[:2], refs[2:]
    else:
        d_out, refs = refs[0], refs[1:]
    kbuf, vbuf, kbuf_t, dbuf, probs, dscores = refs
    n_far = QUAD - 1
    window = QUAD * tok
    quad = meta[0] - meta[0] % QUAD
    z = meta[1]
    shard = (z + n_z - lag) % n_z

    for plane, dst in ((0, kbuf), (1, vbuf)):
        dst[0:n_far * tok, :] = far[plane]
        dst[n_far * tok:, :] = near[plane]
    kbuf_t[...] = kbuf[...].T
    dbuf[...] = d_in[...] if closing else jnp.zeros_like(dbuf)

    def base(group, shard):
        return layout[2 * group + shard // 2] * (2 * tok) + (shard % 2) * tok

    for t, (mask, rows) in enumerate(zip(masks, (rows_a, rows_b))):
        i = member(meta, mask)
        chunk = pl.ds(pl.multiple_of(i * tok, tok), window)
        keys, vals, keys_t = kbuf[chunk, :], vbuf[chunk, :], kbuf_t[:, chunk]
        qbase = base(quad + i, z)
        gaps = [qbase - base((quad + i - n_far + c + n_blk) % n_blk, shard) for c in range(QUAD)]
        row = lax.broadcasted_iota(jnp.int32, (tok, 2 * tok), 0)
        col = lax.broadcasted_iota(jnp.int32, (tok, 2 * tok), 1) % tok
        linked = (col - row + gaps[QUAD - 1]) >= 0

        def stacked(start, heads):
            return jnp.concatenate([rows[start:start + tok, h * HD:(h + 1) * HD] for h in heads], axis=0)

        for g in range(GROUP // 2):
            heads = (2 * g, 2 * g + 1)
            query, dout = stacked(0, heads), stacked(tok, heads)
            span = slice(2 * g * tok, (2 * g + 2) * tok)
            terms = rows[2 * tok:, span].astype(F32)
            lse, delta = terms[0:1] + terms[1:2], terms[2:3] + terms[3:4]
            nt = (((1,), (1,)), ((), ()))
            score = lax.dot_general(keys, query, nt, preferred_element_type=F32) * (SCALE * LOG2E)
            dprob = lax.dot_general(vals, dout, nt, preferred_element_type=F32)
            for c in range(QUAD):
                part = slice(c * tok, (c + 1) * tok)
                if c == QUAD - 1:
                    prob = jnp.where(linked, jnp.exp2(score[part] - lse), 0.0)
                else:
                    prob = jnp.exp2(score[part] - jnp.where(gaps[c] > 0, lse, FAR))
                probs[t, part, span] = prob.astype(BF16)
                dscores[t, part, span] = (prob * (dprob[part] - delta)).astype(BF16)
        query, dout = stacked(0, range(GROUP)), stacked(tok, range(GROUP))
        dbuf[0, chunk, :] += jnp.dot(dscores[t], query, preferred_element_type=F32)
        dbuf[1, chunk, :] += jnp.dot(probs[t], dout, preferred_element_type=F32)
        dq = jnp.dot(keys_t, dscores[t], preferred_element_type=F32)
        if not first:
            dq = dq + acc_in[t]
        if last:
            for h in range(GROUP):
                at = slice(h * HD, (h + 1) * HD)
                dq_outs[t][:, at] = (dq[:, h * tok:(h + 1) * tok] * SCALE).T.astype(BF16)
        else:
            acc_out[t] = dq

    if closing:
        for plane, scale in ((0, SCALE), (1, 1.0)):
            d_far[2 * place + plane] = (dbuf[plane, 0:n_far * tok, :] * scale).astype(BF16)
            d_own[plane] = dbuf[plane, n_far * tok:, :] * scale
    else:
        d_out[...] = dbuf[...]


def attend_call(lag, masks, n_blk, n_z, meta, layout, rows, keys, acc, d_in, after, parts, carried):
    tok = keys[0].shape[1] // QUAD
    first, last, closing = acc is None, lag == n_z - 1, d_in is not None
    chunks = (2 * QUAD - 1) * tok
    near, far = (2, QUAD * tok, HD), (2 * parts, (QUAD - 1) * tok, HD)
    outs = (
        [jax.ShapeDtypeStruct((tok, GROUP * HD), BF16)] * 2
        if last else [jax.ShapeDtypeStruct((2, HD, GROUP * tok), F32)]
    )
    n_heads = len(outs)
    if closing:
        outs = outs + [jax.ShapeDtypeStruct(near, F32), jax.ShapeDtypeStruct(far, BF16)]
    else:
        outs = outs + [jax.ShapeDtypeStruct((2, chunks, HD), F32)]
    inputs = [meta, layout, *rows, *keys]
    aliases = {}
    if not first:
        if not last:
            aliases[len(inputs)] = 0
        inputs.append(acc)
    if closing:
        inputs.append(d_in)
    if carried is not None:
        aliases[len(inputs)] = len(outs) - 1
        after = [carried, *after]
    results = pl.pallas_call(
        functools.partial(
            attend, lag, masks, n_blk, n_z, first, last, closing, len(after), int(carried is not None)
        ),
        out_shape=outs,
        in_specs=[SMEM, SMEM] + [VMEM] * (len(inputs) - 2) + [ANY] * len(after),
        out_specs=[VMEM] * len(outs),
        scratch_shapes=[
            pltpu.VMEM((chunks, HD), BF16),
            pltpu.VMEM((chunks, HD), BF16),
            pltpu.VMEM((HD, chunks), BF16),
            pltpu.VMEM((2, chunks, HD), F32),
            pltpu.VMEM((2, QUAD * tok, GROUP * tok), BF16),
            pltpu.VMEM((2, QUAD * tok, GROUP * tok), BF16),
        ],
        input_output_aliases=aliases,
        compiler_params=pltpu.CompilerParams(vmem_limit_bytes=14 * 2**20),
        cost_estimate=pl.CostEstimate(
            flops=COVER * 4 * tok * GROUP * tok * HD, bytes_accessed=2**20, transcendentals=0
        ),
        name="attend",
    )(*inputs, *after)
    return results[:n_heads], results[n_heads:]


def shards(queries, key_rows, value_rows, attn_out, out_grad, log_norm, block_layout):
    tok = queries.shape[1]
    blk, z = lax.axis_index("blk"), lax.axis_index("head")
    n_blk, n_z = lax.axis_size("blk"), lax.axis_size("head")
    wide = GROUP * HD
    meta = jnp.stack([blk, z]).astype(jnp.int32)
    piece = ((2, tok, HD), BF16)
    ring_of, tail_of = ((2, QUAD * tok, HD), BF16), ((2, (QUAD - 1) * tok, HD), BF16)

    pieces = small_call(pack_kv, [piece] * QUAD, [SMEM, VMEM, VMEM], [meta, key_rows, value_rows])
    parts = [pieces[0]] + [crossed(pieces[mask], mask) for mask in range(1, QUAD)]
    ring, tail = small_call(join_kv, [ring_of, tail_of], [SMEM] + [VMEM] * QUAD, [meta, *parts])
    row_block = ((2 * tok + TERM_ROWS, wide), BF16)
    packed = small_call(
        pack_rows, [row_block] * QUAD, [SMEM] + [VMEM] * 4 + [ANY],
        [meta, queries, out_grad, attn_out, log_norm, pieces[0]],
        scratch=[pltpu.VMEM((log_norm.shape[2], tok), F32)], cost=4 * 2**20,
    )
    rows = [packed[0]] + [crossed(later(packed[mask], [tail]), mask) for mask in range(1, QUAD)]

    keys = [[ring, shifted(tail, "blk", QUAD)]]
    accs = [None, None]
    sums = [None] * n_z

    def pass_keys(after):
        ring, tail = held(shifted(keys[-1][0], "head", 1), after)
        keys.append([ring, shifted(tail, "blk", QUAD)])

    def call(pair, lag, after=(), parts=1, carried=None):
        heads, grads = attend_call(
            lag, (2 * pair, 2 * pair + 1), n_blk, n_z, meta, block_layout, rows[2 * pair:2 * pair + 2], keys[lag],
            accs[pair], sums[lag], after, parts, carried,
        )
        accs[pair] = heads if lag == n_z - 1 else heads[0]
        sums[lag] = grads[0]
        return grads[-1]

    def send_back(grads):
        return shifted(grads, "blk", -QUAD)

    def pass_sums(lag, part, back, packet, after):
        parts = [sums[lag], back, *packet]
        out = small_call(
            functools.partial(pack_sum, part, len(packet)), [ring_of], [VMEM] * len(parts) + [ANY], parts + [after]
        )[0]
        return out, [shifted(out, "head", 1)]

    call(0, 0)
    pass_keys([accs[0]])
    call(0, 1)
    pass_keys([accs[0]])
    call(0, 2)
    pass_keys([accs[0]])
    back_zero = send_back(call(1, 0, [accs[0]]))
    back_one = send_back(call(1, 1))
    back_two = send_back(call(1, 2, [back_zero]))
    _, packet = pass_sums(1, 0, back_one, [], accs[1])
    call(1, 3)
    cross = ((tok, wide + 2 * HD), BF16)
    whole = pltpu.VMEM(ring_of[0], F32)
    sent = small_call(
        functools.partial(pack_cross, (2, 3)), [cross] * 2, [SMEM] + [VMEM] * 4,
        [meta, *accs[1], sums[0], back_zero], scratch=[whole], cost=2**20,
    )
    block, packet = pass_sums(2, 0, back_two, packet, accs[1][0])
    back_three = send_back(call(0, 3, [block]))
    near_half = ((tok, (wide + 2 * HD) // 2), BF16)
    near_one, near_two, kept = small_call(
        pack_near, [near_half] * 2 + [(piece[0], F32)], [SMEM] + [VMEM] * 3 + [ANY],
        [meta, accs[0][1], sums[0], back_zero, *packet], scratch=[whole], cost=2**20,
    )
    near_one, near_two = crossed(near_one, 1), crossed(near_two, 1)
    got = [crossed(part, mask) for mask, part in enumerate(sent, 2)]
    hops = small_call(
        split_sum, [piece] * QUAD, [SMEM] + [VMEM] * 3, [meta, sums[3], back_three, *packet],
        scratch=[pltpu.VMEM(ring_of[0], F32)],
    )
    hops = [hopped(hops[mask], mask) for mask in range(QUAD)]
    query_grad, placed = small_call(
        place_heads, [(queries.shape, BF16), ((8, HD), F32)], [SMEM] + [VMEM] * 5, [meta, accs[0][0], near_one, near_two, *got],
        scratch=[pltpu.SemaphoreType.DMA((5,))], far_out=True,
    )
    flat = (key_rows.shape, BF16)
    key_grad, value_grad = small_call(
        finish, [flat, flat], [SMEM] + [VMEM] * 8 + [ANY], [meta, kept, near_two, *got, *hops, placed]
    )
    return query_grad, key_grad, value_grad


def solution(mesh):
    spread = P("blk", "head", None)
    return jax.shard_map(
        shards,
        mesh=mesh,
        in_specs=(spread,) * 6 + (P(),),
        out_specs=(spread,) * 3,
        check_vma=False,
    )
```

```python
import functools
import math

import jax
import jax.numpy as jnp
from jax import lax
from jax.experimental import pallas as pl
from jax.experimental.pallas import tpu as pltpu
from jax.sharding import PartitionSpec as P

HD = 128
GROUP = 8
QUAD = 4
SCALE = 1.0 / math.sqrt(HD)
LOG2E = math.log2(math.e)
FAR = 1e30
TERM_ROWS = 16
COVER = 12
F32 = jnp.float32
BF16 = jnp.bfloat16
SMEM = pl.BlockSpec(memory_space=pltpu.SMEM)
VMEM = pl.BlockSpec(memory_space=pltpu.VMEM)
ANY = pl.BlockSpec(memory_space=pl.ANY)


def shifted(block, axis, distance):
    size = lax.axis_size(axis)
    route = [((i - distance) % size, i) for i in range(size)]
    return lax.ppermute(block, axis, route)


def crossed(block, mask):
    return lax.ppermute(block, "blk", [(i, i ^ mask) for i in range(lax.axis_size("blk"))])


def hopped(block, mask):
    n_z, n_blk = lax.axis_size("head"), lax.axis_size("blk")
    route = [(i * n_blk + b, (i + 1) % n_z * n_blk + (b ^ mask)) for i in range(n_z) for b in range(n_blk)]
    return lax.ppermute(block, ("head", "blk"), route)


def member(meta, mask):
    c = meta[0] % QUAD
    if mask & 1:
        c = c + 1 - 2 * (c % 2)
    if mask & 2:
        c = (c + 2) % QUAD
    return c


def block_of(meta, mask, size):
    return pl.ds(pl.multiple_of(member(meta, mask) * size, size), size)


def pack_kv(meta, keys, vals, *outs):
    for mask, out in enumerate(outs):
        cols = block_of(meta, mask, HD)
        out[0], out[1] = keys[0, :, cols], vals[0, :, cols]


def join_kv(meta, *refs):
    parts, (ring, tail) = refs[:QUAD], refs[QUAD:]
    tok = parts[0].shape[1]
    for mask, part in enumerate(parts):
        ring[:, block_of(meta, mask, tok), :] = part[...]
    tail[...] = ring[:, tok:, :]


def pack_rows(meta, queries, douts, outs, lse, _, *refs):
    packed, lse_t = refs[:QUAD], refs[QUAD]
    tok = queries.shape[1]
    wide = GROUP * HD
    lse_t[...] = lse[0].T * LOG2E
    for mask, out in enumerate(packed):
        cols = block_of(meta, mask, wide)
        out[0:tok, :] = queries[0, :, cols]
        out[tok:2 * tok, :] = douts[0, :, cols]
        norms = lse_t[block_of(meta, mask, GROUP), :]
        for h in range(GROUP):
            at = slice(h * HD, (h + 1) * HD)
            head = pl.ds(pl.multiple_of(member(meta, mask) * wide + h * HD, HD), HD)
            prod = out[tok:2 * tok, at].astype(F32) * outs[0, :, head].astype(F32)
            delta = jnp.sum(prod.T, axis=0, keepdims=True)
            lines = []
            for term in (norms[h:h + 1], delta):
                high = term.astype(BF16).astype(F32)
                lines += [high, term - high]
            block = jnp.concatenate(lines + [jnp.zeros((TERM_ROWS - 4, tok), F32)], axis=0).astype(BF16)
            out[2 * tok:, h * tok:(h + 1) * tok] = block


def do_nothing(*refs):
    del refs


def later(block, after=(), cost=0):
    return pl.pallas_call(
        do_nothing,
        out_shape=jax.ShapeDtypeStruct(block.shape, block.dtype),
        in_specs=[ANY] * (1 + len(after)),
        out_specs=ANY,
        input_output_aliases={0: 0},
        compiler_params=pltpu.CompilerParams(vmem_limit_bytes=2**20),
        cost_estimate=pl.CostEstimate(flops=cost, bytes_accessed=0, transcendentals=0),
        name="later",
    )(block, *after)


def pass_on(ring_in, *refs):
    tail = refs[-1]
    tail[...] = ring_in[:, ring_in.shape[1] - tail.shape[1]:, :]


def held(ring, after):
    planes, rows, cols = ring.shape
    return pl.pallas_call(
        pass_on,
        out_shape=[
            jax.ShapeDtypeStruct(ring.shape, ring.dtype),
            jax.ShapeDtypeStruct((planes, rows // QUAD * (QUAD - 1), cols), ring.dtype),
        ],
        in_specs=[VMEM] + [ANY] * len(after),
        out_specs=[ANY, VMEM],
        input_output_aliases={0: 0},
        compiler_params=pltpu.CompilerParams(vmem_limit_bytes=4 * 2**20),
        name="pass_on",
    )(ring, *after)


def side_by_side(first, second, out):
    out[0:2] = first[...]
    out[2:4] = second[...]


def total(part, n_packet, d_own, back, refs):
    tok = d_own.shape[1] // QUAD
    tail = d_own[:, tok:, :] + back[2 * part:2 * part + 2].astype(F32)
    lead = d_own[:, 0:tok, :]
    if n_packet:
        lead += refs[0][:, 0:tok, :].astype(F32)
        tail += refs[0][:, tok:, :].astype(F32)
    return lead, tail


def pack_sum(part, n_packet, d_own, back, *refs):
    lead, tail = total(part, n_packet, d_own, back, refs)
    out = refs[-1]
    tok = lead.shape[1]
    out[:, 0:tok, :] = lead.astype(BF16)
    out[:, tok:, :] = tail.astype(BF16)


def split_sum(meta, d_own, back, packet, *refs):
    outs, whole = refs[:QUAD], refs[QUAD]
    lead, tail = total(0, 1, d_own, back, (packet,))
    tok = lead.shape[1]
    whole[:, 0:tok, :] = lead
    whole[:, tok:, :] = tail
    for mask, out in enumerate(outs):
        out[...] = whole[:, block_of(meta, mask, tok), :].astype(BF16)


def pack_cross(masks, meta, *refs):
    n = len(masks)
    dqs, (d_own, back), outs, whole = refs[:n], refs[n:n + 2], refs[n + 2:-1], refs[-1]
    lead, tail = total(1, 0, d_own, back, ())
    tok, wide = dqs[0].shape
    whole[:, 0:tok, :] = lead
    whole[:, tok:, :] = tail
    for mask, dq, out in zip(masks, dqs, outs):
        out[:, 0:wide] = dq[...]
        part = whole[:, block_of(meta, mask, tok), :].astype(BF16)
        out[:, wide:wide + HD] = part[0]
        out[:, wide + HD:] = part[1]


def pack_near(meta, dq, d_own, back, first, second, kept, whole):
    lead, tail = total(1, 0, d_own, back, ())
    tok, wide = dq.shape
    half = first.shape[1]
    whole[:, 0:tok, :] = lead
    whole[:, tok:, :] = tail
    part = whole[:, block_of(meta, 1, tok), :].astype(BF16)
    first[...] = dq[:, 0:half]
    second[:, 0:wide - half] = dq[:, half:]
    second[:, wide - half:wide - half + HD] = part[0]
    second[:, wide - half + HD:] = part[1]
    kept[...] = whole[:, block_of(meta, 0, tok), :]


def place_heads(meta, dq_own, near_one, near_two, got_two, got_three, out, done, sems):
    wide = dq_own.shape[1]
    half = near_one.shape[1]
    copies = []
    for mask, src in ((0, dq_own), (2, got_two.at[:, 0:wide]), (3, got_three.at[:, 0:wide])):
        copies.append(pltpu.make_async_copy(src, out.at[0, :, block_of(meta, mask, wide)], sems.at[len(copies)]))
    for start, src in ((0, near_one), (half, near_two.at[:, 0:wide - half])):
        cols = pl.ds(pl.multiple_of(member(meta, 1) * wide + start, HD), src.shape[1])
        copies.append(pltpu.make_async_copy(src, out.at[0, :, cols], sems.at[len(copies)]))
    for copy in copies:
        copy.start()
    done[...] = jnp.zeros_like(done)
    for copy in copies:
        copy.wait()


def finish(meta, kept, near_two, got_two, got_three, hop0, hop1, hop2, hop3, _, dkey, dval):
    for mask, (got, hop) in enumerate(zip((kept, near_two, got_two, got_three), (hop0, hop1, hop2, hop3))):
        cols = block_of(meta, mask, HD)
        for plane, dst in ((0, dkey), (1, dval)):
            if mask == 0:
                first = got[plane]
            else:
                start = got.shape[1] - (2 - plane) * HD
                first = got[:, start:start + HD].astype(F32)
            dst[0, :, cols] = (first + hop[plane].astype(F32)).astype(BF16)


def small_call(body, outs, specs, operands, scratch=(), cost=0, far_out=False):
    shapes = [jax.ShapeDtypeStruct(shape, kind) for shape, kind in outs]
    name = getattr(body, "func", body).__name__
    return pl.pallas_call(
        body,
        out_shape=shapes,
        in_specs=specs,
        out_specs=[ANY if i == 0 and far_out else VMEM for i in range(len(shapes))],
        scratch_shapes=list(scratch),
        compiler_params=pltpu.CompilerParams(vmem_limit_bytes=4 * 2**20),
        cost_estimate=pl.CostEstimate(flops=0, bytes_accessed=cost, transcendentals=0),
        name=name,
    )(*operands)


def attend(lag, masks, n_blk, n_z, first, last, closing, n_after, place, meta, layout, *refs):
    (rows_a, rows_b, near, far), refs = refs[:4], refs[4:]
    tok = near.shape[1] // QUAD
    if not first:
        acc_in, refs = refs[0], refs[1:]
    if closing:
        d_in, refs = refs[0], refs[1:]
    refs = refs[n_after:]
    if last:
        dq_outs, refs = refs[:2], refs[2:]
    else:
        acc_out, refs = refs[0], refs[1:]
    if closing:
        (d_own, d_far), refs = refs[:2], refs[2:]
    else:
        d_out, refs = refs[0], refs[1:]
    kbuf, vbuf, kbuf_t, dbuf, probs, dscores = refs
    n_far = QUAD - 1
    window = QUAD * tok
    quad = meta[0] - meta[0] % QUAD
    z = meta[1]
    shard = (z + n_z - lag) % n_z

    for plane, dst in ((0, kbuf), (1, vbuf)):
        dst[0:n_far * tok, :] = far[plane]
        dst[n_far * tok:, :] = near[plane]
    kbuf_t[...] = kbuf[...].T
    dbuf[...] = d_in[...] if closing else jnp.zeros_like(dbuf)

    def base(group, shard):
        return layout[2 * group + shard // 2] * (2 * tok) + (shard % 2) * tok

    sets = []
    for mask, rows in zip(masks, (rows_a, rows_b)):
        i = member(meta, mask)
        chunk = pl.ds(pl.multiple_of(i * tok, tok), window)
        qbase = base(quad + i, z)
        gaps = [qbase - base((quad + i - n_far + c + n_blk) % n_blk, shard) for c in range(QUAD)]
        sets.append((rows, chunk, gaps))
    row = lax.broadcasted_iota(jnp.int32, (tok, 2 * tok), 0)
    col = lax.broadcasted_iota(jnp.int32, (tok, 2 * tok), 1) % tok
    nt = (((1,), (1,)), ((), ()))
    half = GROUP // 2
    steps = [(t, part) for t in range(2) for part in range(2)]
    scores = {}

    def stacked(rows, start, heads):
        return jnp.concatenate([rows[start:start + tok, h * HD:(h + 1) * HD] for h in heads], axis=0)

    def score_part(t, part):
        rows, chunk, _ = sets[t]
        keys, vals = kbuf[chunk, :], vbuf[chunk, :]
        for g in range(part * half, (part + 1) * half, 2):
            query, dout = stacked(rows, 0, (g, g + 1)), stacked(rows, tok, (g, g + 1))
            scores[t, g] = (
                lax.dot_general(keys, query, nt, preferred_element_type=F32),
                lax.dot_general(vals, dout, nt, preferred_element_type=F32),
            )

    def prob_part(t, part):
        rows, _, gaps = sets[t]
        linked = (col - row + gaps[QUAD - 1]) >= 0
        for g in range(part * half, (part + 1) * half, 2):
            score, dprob = scores.pop((t, g))
            span = slice(g * tok, (g + 2) * tok)
            terms = rows[2 * tok:, span].astype(F32)
            lse, delta = terms[0:1] + terms[1:2], terms[2:3] + terms[3:4]
            for c in range(QUAD):
                at = slice(c * tok, (c + 1) * tok)
                scaled = score[at] * (SCALE * LOG2E)
                if c == QUAD - 1:
                    prob = jnp.where(linked, jnp.exp2(scaled - lse), 0.0)
                else:
                    prob = jnp.exp2(scaled - jnp.where(gaps[c] > 0, lse, FAR))
                probs[t, at, span] = prob.astype(BF16)
                dscores[t, at, span] = (prob * (dprob[at] - delta)).astype(BF16)

    def grad_part(t, part):
        rows, chunk, _ = sets[t]
        heads = range(part * half, (part + 1) * half)
        query, dout = stacked(rows, 0, heads), stacked(rows, tok, heads)
        span = slice(part * half * tok, (part + 1) * half * tok)
        dbuf[0, chunk, :] += jnp.dot(dscores[t, :, span], query, preferred_element_type=F32)
        dbuf[1, chunk, :] += jnp.dot(probs[t, :, span], dout, preferred_element_type=F32)
        dq = jnp.dot(kbuf_t[:, chunk], dscores[t, :, span], preferred_element_type=F32)
        if not first:
            dq = dq + acc_in[t, :, span]
        if last:
            for n, h in enumerate(heads):
                at = slice(h * HD, (h + 1) * HD)
                dq_outs[t][:, at] = (dq[:, n * tok:(n + 1) * tok] * SCALE).T.astype(BF16)
        else:
            acc_out[t, :, span] = dq

    for n in range(len(steps) + 2):
        if n < len(steps):
            score_part(*steps[n])
        if 1 <= n <= len(steps):
            prob_part(*steps[n - 1])
        if n >= 2:
            grad_part(*steps[n - 2])

    if closing:
        for plane, scale in ((0, SCALE), (1, 1.0)):
            d_far[2 * place + plane] = (dbuf[plane, 0:n_far * tok, :] * scale).astype(BF16)
            d_own[plane] = dbuf[plane, n_far * tok:, :] * scale
    else:
        d_out[...] = dbuf[...]


def attend_call(lag, masks, n_blk, n_z, meta, layout, rows, keys, acc, d_in, after, parts, carried):
    tok = keys[0].shape[1] // QUAD
    first, last, closing = acc is None, lag == n_z - 1, d_in is not None
    chunks = (2 * QUAD - 1) * tok
    near, far = (2, QUAD * tok, HD), (2 * parts, (QUAD - 1) * tok, HD)
    outs = (
        [jax.ShapeDtypeStruct((tok, GROUP * HD), BF16)] * 2
        if last else [jax.ShapeDtypeStruct((2, HD, GROUP * tok), F32)]
    )
    n_heads = len(outs)
    if closing:
        outs = outs + [jax.ShapeDtypeStruct(near, F32), jax.ShapeDtypeStruct(far, BF16)]
    else:
        outs = outs + [jax.ShapeDtypeStruct((2, chunks, HD), F32)]
    inputs = [meta, layout, *rows, *keys]
    aliases = {}
    if not first:
        if not last:
            aliases[len(inputs)] = 0
        inputs.append(acc)
    if closing:
        inputs.append(d_in)
    if carried is not None:
        aliases[len(inputs)] = len(outs) - 1
        after = [carried, *after]
    results = pl.pallas_call(
        functools.partial(
            attend, lag, masks, n_blk, n_z, first, last, closing, len(after), int(carried is not None)
        ),
        out_shape=outs,
        in_specs=[SMEM, SMEM] + [VMEM] * (len(inputs) - 2) + [ANY] * len(after),
        out_specs=[VMEM] * len(outs),
        scratch_shapes=[
            pltpu.VMEM((chunks, HD), BF16),
            pltpu.VMEM((chunks, HD), BF16),
            pltpu.VMEM((HD, chunks), BF16),
            pltpu.VMEM((2, chunks, HD), F32),
            pltpu.VMEM((2, QUAD * tok, GROUP * tok), BF16),
            pltpu.VMEM((2, QUAD * tok, GROUP * tok), BF16),
        ],
        input_output_aliases=aliases,
        compiler_params=pltpu.CompilerParams(vmem_limit_bytes=18 * 2**20),
        cost_estimate=pl.CostEstimate(
            flops=COVER * 4 * tok * GROUP * tok * HD, bytes_accessed=2**20, transcendentals=0
        ),
        name="attend",
    )(*inputs, *after)
    return results[:n_heads], results[n_heads:]


def shards(queries, key_rows, value_rows, attn_out, out_grad, log_norm, block_layout):
    tok = queries.shape[1]
    blk, z = lax.axis_index("blk"), lax.axis_index("head")
    n_blk, n_z = lax.axis_size("blk"), lax.axis_size("head")
    wide = GROUP * HD
    meta = jnp.stack([blk, z]).astype(jnp.int32)
    piece = ((2, tok, HD), BF16)
    ring_of, tail_of = ((2, QUAD * tok, HD), BF16), ((2, (QUAD - 1) * tok, HD), BF16)

    pieces = small_call(pack_kv, [piece] * QUAD, [SMEM, VMEM, VMEM], [meta, key_rows, value_rows])
    parts = [pieces[0]] + [crossed(pieces[mask], mask) for mask in range(1, QUAD)]
    ring, tail = small_call(join_kv, [ring_of, tail_of], [SMEM] + [VMEM] * QUAD, [meta, *parts])
    row_block = ((2 * tok + TERM_ROWS, wide), BF16)
    packed = small_call(
        pack_rows, [row_block] * QUAD, [SMEM] + [VMEM] * 4 + [ANY],
        [meta, queries, out_grad, attn_out, log_norm, pieces[0]],
        scratch=[pltpu.VMEM((log_norm.shape[2], tok), F32)], cost=4 * 2**20,
    )
    rows = [packed[0]] + [crossed(later(packed[mask], [tail]), mask) for mask in range(1, QUAD)]

    keys = [[ring, shifted(tail, "blk", QUAD)]]
    accs = [None, None]
    sums = [None] * n_z

    def pass_keys(after):
        ring, tail = held(shifted(keys[-1][0], "head", 1), after)
        keys.append([ring, shifted(tail, "blk", QUAD)])

    def keys_and_back(tail, grads):
        pair = ((4, *tail_of[0][1:]), BF16)
        if n_blk != 2 * QUAD:
            tail, grads = shifted(tail, "blk", QUAD), shifted(grads, "blk", -QUAD)
        both = small_call(side_by_side, [pair], [VMEM] * 2, [tail, grads])[0]
        return shifted(both, "blk", QUAD) if n_blk == 2 * QUAD else both

    def call(pair, lag, after=(), parts=1, carried=None):
        heads, grads = attend_call(
            lag, (2 * pair, 2 * pair + 1), n_blk, n_z, meta, block_layout, rows[2 * pair:2 * pair + 2], keys[lag],
            accs[pair], sums[lag], after, parts, carried,
        )
        accs[pair] = heads if lag == n_z - 1 else heads[0]
        sums[lag] = grads[0]
        return grads[-1]

    def send_back(grads):
        return shifted(grads, "blk", -QUAD)

    def pass_sums(lag, part, back, packet, after):
        parts = [sums[lag], back, *packet]
        out = small_call(
            functools.partial(pack_sum, part, len(packet)), [ring_of], [VMEM] * len(parts) + [ANY], parts + [after]
        )[0]
        return out, [shifted(out, "head", 1)]

    call(0, 0)
    pass_keys([accs[0]])
    call(0, 1)
    pass_keys([accs[0]])
    call(0, 2)
    ring, tail = held(shifted(keys[-1][0], "head", 1), [accs[0]])
    back_zero = keys_and_back(tail, call(1, 0, [accs[0]]))
    keys.append([ring, back_zero])
    back_one = send_back(call(1, 1))
    back_two = send_back(call(1, 2))
    call(1, 3)
    _, packet = pass_sums(1, 0, back_one, [], accs[1][0])
    cross = ((tok, wide + 2 * HD), BF16)
    whole = pltpu.VMEM(ring_of[0], F32)
    sent = small_call(
        functools.partial(pack_cross, (2, 3)), [cross] * 2, [SMEM] + [VMEM] * 4,
        [meta, *accs[1], sums[0], back_zero], scratch=[whole], cost=2**20,
    )
    back_three = send_back(call(0, 3, [accs[1][0], sent[0], back_two]))
    _, packet = pass_sums(2, 0, back_two, packet, sums[3])
    near_half = ((tok, (wide + 2 * HD) // 2), BF16)
    near_one, near_two, kept = small_call(
        pack_near, [near_half] * 2 + [(piece[0], F32)], [SMEM] + [VMEM] * 3,
        [meta, accs[0][1], sums[0], back_zero], scratch=[whole], cost=2**20,
    )
    near_one, near_two = crossed(near_one, 1), crossed(near_two, 1)
    got = [crossed(part, mask) for mask, part in enumerate(sent, 2)]
    hops = small_call(
        split_sum, [piece] * QUAD, [SMEM] + [VMEM] * 3, [meta, sums[3], back_three, *packet],
        scratch=[pltpu.VMEM(ring_of[0], F32)],
    )
    hops = [hopped(hops[mask], mask) for mask in range(QUAD)]
    query_grad, placed = small_call(
        place_heads, [(queries.shape, BF16), ((8, HD), F32)], [SMEM] + [VMEM] * 5, [meta, accs[0][0], near_one, near_two, *got],
        scratch=[pltpu.SemaphoreType.DMA((5,))], far_out=True,
    )
    flat = (key_rows.shape, BF16)
    key_grad, value_grad = small_call(
        finish, [flat, flat], [SMEM] + [VMEM] * 8 + [ANY], [meta, kept, near_two, *got, *hops, placed]
    )
    return query_grad, key_grad, value_grad


def solution(mesh):
    spread = P("blk", "head", None)
    return jax.shard_map(
        shards,
        mesh=mesh,
        in_specs=(spread,) * 6 + (P(),),
        out_specs=(spread,) * 3,
        check_vma=False,
    )
```

```python
import functools
import math

import jax
import jax.numpy as jnp
from jax import lax
from jax.experimental import pallas as pl
from jax.experimental.pallas import tpu as pltpu
from jax.sharding import PartitionSpec as P

HD = 128
GROUP = 8
QUAD = 4
SCALE = 1.0 / math.sqrt(HD)
LOG2E = math.log2(math.e)
FAR = 1e30
TERM_ROWS = 16
COVER = 12
F32 = jnp.float32
BF16 = jnp.bfloat16
SMEM = pl.BlockSpec(memory_space=pltpu.SMEM)
VMEM = pl.BlockSpec(memory_space=pltpu.VMEM)
ANY = pl.BlockSpec(memory_space=pl.ANY)


def shifted(block, axis, distance):
    size = lax.axis_size(axis)
    route = [((i - distance) % size, i) for i in range(size)]
    return lax.ppermute(block, axis, route)


def crossed(block, mask):
    return lax.ppermute(block, "blk", [(i, i ^ mask) for i in range(lax.axis_size("blk"))])


def hopped(block, mask):
    n_z, n_blk = lax.axis_size("head"), lax.axis_size("blk")
    route = [(i * n_blk + b, (i + 1) % n_z * n_blk + (b ^ mask)) for i in range(n_z) for b in range(n_blk)]
    return lax.ppermute(block, ("head", "blk"), route)


def member(meta, mask):
    c = meta[0] % QUAD
    if mask & 1:
        c = c + 1 - 2 * (c % 2)
    if mask & 2:
        c = (c + 2) % QUAD
    return c


def block_of(meta, mask, size):
    return pl.ds(pl.multiple_of(member(meta, mask) * size, size), size)


def pack_kv(meta, keys, vals, *outs):
    for mask, out in enumerate(outs):
        cols = block_of(meta, mask, HD)
        out[0], out[1] = keys[0, :, cols], vals[0, :, cols]


def join_kv(meta, *refs):
    parts, (ring, tail) = refs[:QUAD], refs[QUAD:]
    tok = parts[0].shape[1]
    for mask, part in enumerate(parts):
        ring[:, block_of(meta, mask, tok), :] = part[...]
    tail[...] = ring[:, tok:, :]


def pack_rows(meta, queries, douts, outs, lse, _, *refs):
    packed, lse_t = refs[:QUAD], refs[QUAD]
    tok = queries.shape[1]
    wide = GROUP * HD
    lse_t[...] = lse[0].T * LOG2E
    for mask, out in enumerate(packed):
        cols = block_of(meta, mask, wide)
        out[0:tok, :] = queries[0, :, cols]
        out[tok:2 * tok, :] = douts[0, :, cols]
        norms = lse_t[block_of(meta, mask, GROUP), :]
        for h in range(GROUP):
            at = slice(h * HD, (h + 1) * HD)
            head = pl.ds(pl.multiple_of(member(meta, mask) * wide + h * HD, HD), HD)
            prod = out[tok:2 * tok, at].astype(F32) * outs[0, :, head].astype(F32)
            delta = jnp.sum(prod.T, axis=0, keepdims=True)
            lines = []
            for term in (norms[h:h + 1], delta):
                high = term.astype(BF16).astype(F32)
                lines += [high, term - high]
            block = jnp.concatenate(lines + [jnp.zeros((TERM_ROWS - 4, tok), F32)], axis=0).astype(BF16)
            out[2 * tok:, h * tok:(h + 1) * tok] = block


def do_nothing(*refs):
    del refs


def later(block, after=(), cost=0):
    return pl.pallas_call(
        do_nothing,
        out_shape=jax.ShapeDtypeStruct(block.shape, block.dtype),
        in_specs=[ANY] * (1 + len(after)),
        out_specs=ANY,
        input_output_aliases={0: 0},
        compiler_params=pltpu.CompilerParams(vmem_limit_bytes=2**20),
        cost_estimate=pl.CostEstimate(flops=cost, bytes_accessed=0, transcendentals=0),
        name="later",
    )(block, *after)


def pass_on(ring_in, *refs):
    tail = refs[-1]
    tail[...] = ring_in[:, ring_in.shape[1] - tail.shape[1]:, :]


def held(ring, after):
    planes, rows, cols = ring.shape
    return pl.pallas_call(
        pass_on,
        out_shape=[
            jax.ShapeDtypeStruct(ring.shape, ring.dtype),
            jax.ShapeDtypeStruct((planes, rows // QUAD * (QUAD - 1), cols), ring.dtype),
        ],
        in_specs=[VMEM] + [ANY] * len(after),
        out_specs=[ANY, VMEM],
        input_output_aliases={0: 0},
        compiler_params=pltpu.CompilerParams(vmem_limit_bytes=4 * 2**20),
        name="pass_on",
    )(ring, *after)


def side_by_side(first, second, out):
    out[0:2] = first[...]
    out[2:4] = second[...]


def total(part, n_packet, d_own, back, refs):
    tok = d_own.shape[1] // QUAD
    tail = d_own[:, tok:, :] + back[2 * part:2 * part + 2].astype(F32)
    lead = d_own[:, 0:tok, :]
    for packet in refs[:n_packet]:
        lead += packet[:, 0:tok, :].astype(F32)
        tail += packet[:, tok:, :].astype(F32)
    return lead, tail


def pack_sum(d_own, back, _, out):
    lead, tail = total(0, 0, d_own, back, ())
    tok = lead.shape[1]
    out[:, 0:tok, :] = lead.astype(BF16)
    out[:, tok:, :] = tail.astype(BF16)


def split_sum(meta, d_own, back, packet_one, packet_two, *refs):
    outs, whole = refs[:QUAD], refs[QUAD]
    lead, tail = total(0, 2, d_own, back, (packet_one, packet_two))
    tok = lead.shape[1]
    whole[:, 0:tok, :] = lead
    whole[:, tok:, :] = tail
    for mask, out in enumerate(outs):
        out[...] = whole[:, block_of(meta, mask, tok), :].astype(BF16)


def pack_cross(masks, meta, *refs):
    n = len(masks)
    dqs, (d_own, back), outs, whole = refs[:n], refs[n:n + 2], refs[n + 2:-1], refs[-1]
    lead, tail = total(1, 0, d_own, back, ())
    tok, wide = dqs[0].shape
    whole[:, 0:tok, :] = lead
    whole[:, tok:, :] = tail
    for mask, dq, out in zip(masks, dqs, outs):
        out[:, 0:wide] = dq[...]
        part = whole[:, block_of(meta, mask, tok), :].astype(BF16)
        out[:, wide:wide + HD] = part[0]
        out[:, wide + HD:] = part[1]


def pack_near(meta, dq, d_own, back, *refs):
    first, second, kept, whole = refs[-4:]
    lead, tail = total(1, 0, d_own, back, ())
    tok, wide = dq.shape
    half = first.shape[1]
    whole[:, 0:tok, :] = lead
    whole[:, tok:, :] = tail
    part = whole[:, block_of(meta, 1, tok), :].astype(BF16)
    first[...] = dq[:, 0:half]
    second[:, 0:wide - half] = dq[:, half:]
    second[:, wide - half:wide - half + HD] = part[0]
    second[:, wide - half + HD:] = part[1]
    kept[...] = whole[:, block_of(meta, 0, tok), :]


def place_heads(meta, dq_own, near_one, near_two, got_two, got_three, out, done, sems):
    wide = dq_own.shape[1]
    half = near_one.shape[1]
    copies = []
    for mask, src in ((0, dq_own), (2, got_two.at[:, 0:wide]), (3, got_three.at[:, 0:wide])):
        copies.append(pltpu.make_async_copy(src, out.at[0, :, block_of(meta, mask, wide)], sems.at[len(copies)]))
    for start, src in ((0, near_one), (half, near_two.at[:, 0:wide - half])):
        cols = pl.ds(pl.multiple_of(member(meta, 1) * wide + start, HD), src.shape[1])
        copies.append(pltpu.make_async_copy(src, out.at[0, :, cols], sems.at[len(copies)]))
    for copy in copies:
        copy.start()
    done[...] = jnp.zeros_like(done)
    for copy in copies:
        copy.wait()


def finish(meta, kept, near_two, got_two, got_three, hop0, hop1, hop2, hop3, _, dkey, dval):
    for mask, (got, hop) in enumerate(zip((kept, near_two, got_two, got_three), (hop0, hop1, hop2, hop3))):
        cols = block_of(meta, mask, HD)
        for plane, dst in ((0, dkey), (1, dval)):
            if mask == 0:
                first = got[plane]
            else:
                start = got.shape[1] - (2 - plane) * HD
                first = got[:, start:start + HD].astype(F32)
            dst[0, :, cols] = (first + hop[plane].astype(F32)).astype(BF16)


def small_call(body, outs, specs, operands, scratch=(), cost=0, far_out=False):
    shapes = [jax.ShapeDtypeStruct(shape, kind) for shape, kind in outs]
    name = getattr(body, "func", body).__name__
    return pl.pallas_call(
        body,
        out_shape=shapes,
        in_specs=specs,
        out_specs=[ANY if i == 0 and far_out else VMEM for i in range(len(shapes))],
        scratch_shapes=list(scratch),
        compiler_params=pltpu.CompilerParams(vmem_limit_bytes=4 * 2**20),
        cost_estimate=pl.CostEstimate(flops=0, bytes_accessed=cost, transcendentals=0),
        name=name,
    )(*operands)


def attend(lag, masks, n_blk, n_z, first, last, closing, n_after, place, meta, layout, *refs):
    (rows_a, rows_b, near, far), refs = refs[:4], refs[4:]
    tok = near.shape[1] // QUAD
    if not first:
        acc_in, refs = refs[0], refs[1:]
    if closing:
        d_in, refs = refs[0], refs[1:]
    refs = refs[n_after:]
    if last:
        dq_outs, refs = refs[:2], refs[2:]
    else:
        acc_out, refs = refs[0], refs[1:]
    if closing:
        (d_own, d_far), refs = refs[:2], refs[2:]
    else:
        d_out, refs = refs[0], refs[1:]
    kbuf, vbuf, kbuf_t, dbuf, probs, dscores = refs
    n_far = QUAD - 1
    window = QUAD * tok
    quad = meta[0] - meta[0] % QUAD
    z = meta[1]
    shard = (z + n_z - lag) % n_z

    for plane, dst in ((0, kbuf), (1, vbuf)):
        dst[0:n_far * tok, :] = far[plane]
        dst[n_far * tok:, :] = near[plane]
    kbuf_t[...] = kbuf[...].T
    dbuf[...] = d_in[...] if closing else jnp.zeros_like(dbuf)

    def base(group, shard):
        return layout[2 * group + shard // 2] * (2 * tok) + (shard % 2) * tok

    sets = []
    for mask, rows in zip(masks, (rows_a, rows_b)):
        i = member(meta, mask)
        chunk = pl.ds(pl.multiple_of(i * tok, tok), window)
        qbase = base(quad + i, z)
        gaps = [qbase - base((quad + i - n_far + c + n_blk) % n_blk, shard) for c in range(QUAD)]
        sets.append((rows, chunk, gaps))
    row = lax.broadcasted_iota(jnp.int32, (tok, 2 * tok), 0)
    col = lax.broadcasted_iota(jnp.int32, (tok, 2 * tok), 1) % tok
    nt = (((1,), (1,)), ((), ()))
    half = GROUP // 2
    steps = [(t, part) for t in range(2) for part in range(2)]
    scores = {}

    def stacked(rows, start, heads):
        return jnp.concatenate([rows[start:start + tok, h * HD:(h + 1) * HD] for h in heads], axis=0)

    def score_part(t, part):
        rows, chunk, _ = sets[t]
        keys, vals = kbuf[chunk, :], vbuf[chunk, :]
        for g in range(part * half, (part + 1) * half, 2):
            query, dout = stacked(rows, 0, (g, g + 1)), stacked(rows, tok, (g, g + 1))
            scores[t, g] = (
                lax.dot_general(keys, query, nt, preferred_element_type=F32),
                lax.dot_general(vals, dout, nt, preferred_element_type=F32),
            )

    def prob_part(t, part):
        rows, _, gaps = sets[t]
        linked = (col - row + gaps[QUAD - 1]) >= 0
        for g in range(part * half, (part + 1) * half, 2):
            score, dprob = scores.pop((t, g))
            span = slice(g * tok, (g + 2) * tok)
            terms = rows[2 * tok:, span].astype(F32)
            lse, delta = terms[0:1] + terms[1:2], terms[2:3] + terms[3:4]
            for c in range(QUAD):
                at = slice(c * tok, (c + 1) * tok)
                scaled = score[at] * (SCALE * LOG2E)
                if c == QUAD - 1:
                    prob = jnp.where(linked, jnp.exp2(scaled - lse), 0.0)
                else:
                    prob = jnp.exp2(scaled - jnp.where(gaps[c] > 0, lse, FAR))
                probs[t, at, span] = prob.astype(BF16)
                dscores[t, at, span] = (prob * (dprob[at] - delta)).astype(BF16)

    def grad_part(t, part):
        rows, chunk, _ = sets[t]
        heads = range(part * half, (part + 1) * half)
        query, dout = stacked(rows, 0, heads), stacked(rows, tok, heads)
        span = slice(part * half * tok, (part + 1) * half * tok)
        dbuf[0, chunk, :] += jnp.dot(dscores[t, :, span], query, preferred_element_type=F32)
        dbuf[1, chunk, :] += jnp.dot(probs[t, :, span], dout, preferred_element_type=F32)
        dq = jnp.dot(kbuf_t[:, chunk], dscores[t, :, span], preferred_element_type=F32)
        if not first:
            dq = dq + acc_in[t, :, span]
        if last:
            for n, h in enumerate(heads):
                at = slice(h * HD, (h + 1) * HD)
                dq_outs[t][:, at] = (dq[:, n * tok:(n + 1) * tok] * SCALE).T.astype(BF16)
        else:
            acc_out[t, :, span] = dq

    for n in range(len(steps) + 2):
        if n < len(steps):
            score_part(*steps[n])
        if 1 <= n <= len(steps):
            prob_part(*steps[n - 1])
        if n >= 2:
            grad_part(*steps[n - 2])

    if closing:
        for plane, scale in ((0, SCALE), (1, 1.0)):
            d_far[2 * place + plane] = (dbuf[plane, 0:n_far * tok, :] * scale).astype(BF16)
            d_own[plane] = dbuf[plane, n_far * tok:, :] * scale
    else:
        d_out[...] = dbuf[...]


def attend_call(lag, masks, n_blk, n_z, meta, layout, rows, keys, acc, d_in, after, parts, carried):
    tok = keys[0].shape[1] // QUAD
    first, last, closing = acc is None, lag == n_z - 1, d_in is not None
    chunks = (2 * QUAD - 1) * tok
    near, far = (2, QUAD * tok, HD), (2 * parts, (QUAD - 1) * tok, HD)
    outs = (
        [jax.ShapeDtypeStruct((tok, GROUP * HD), BF16)] * 2
        if last else [jax.ShapeDtypeStruct((2, HD, GROUP * tok), F32)]
    )
    n_heads = len(outs)
    if closing:
        outs = outs + [jax.ShapeDtypeStruct(near, F32), jax.ShapeDtypeStruct(far, BF16)]
    else:
        outs = outs + [jax.ShapeDtypeStruct((2, chunks, HD), F32)]
    inputs = [meta, layout, *rows, *keys]
    aliases = {}
    if not first:
        if not last:
            aliases[len(inputs)] = 0
        inputs.append(acc)
    if closing:
        inputs.append(d_in)
    if carried is not None:
        aliases[len(inputs)] = len(outs) - 1
        after = [carried, *after]
    results = pl.pallas_call(
        functools.partial(
            attend, lag, masks, n_blk, n_z, first, last, closing, len(after), int(carried is not None)
        ),
        out_shape=outs,
        in_specs=[SMEM, SMEM] + [VMEM] * (len(inputs) - 2) + [ANY] * len(after),
        out_specs=[VMEM] * len(outs),
        scratch_shapes=[
            pltpu.VMEM((chunks, HD), BF16),
            pltpu.VMEM((chunks, HD), BF16),
            pltpu.VMEM((HD, chunks), BF16),
            pltpu.VMEM((2, chunks, HD), F32),
            pltpu.VMEM((2, QUAD * tok, GROUP * tok), BF16),
            pltpu.VMEM((2, QUAD * tok, GROUP * tok), BF16),
        ],
        input_output_aliases=aliases,
        compiler_params=pltpu.CompilerParams(vmem_limit_bytes=18 * 2**20),
        cost_estimate=pl.CostEstimate(
            flops=COVER * 4 * tok * GROUP * tok * HD, bytes_accessed=2**20, transcendentals=0
        ),
        name="attend",
    )(*inputs, *after)
    return results[:n_heads], results[n_heads:]


def shards(queries, key_rows, value_rows, attn_out, out_grad, log_norm, block_layout):
    tok = queries.shape[1]
    blk, z = lax.axis_index("blk"), lax.axis_index("head")
    n_blk, n_z = lax.axis_size("blk"), lax.axis_size("head")
    wide = GROUP * HD
    meta = jnp.stack([blk, z]).astype(jnp.int32)
    piece = ((2, tok, HD), BF16)
    ring_of, tail_of = ((2, QUAD * tok, HD), BF16), ((2, (QUAD - 1) * tok, HD), BF16)

    pieces = small_call(pack_kv, [piece] * QUAD, [SMEM, VMEM, VMEM], [meta, key_rows, value_rows])
    parts = [pieces[0]] + [crossed(pieces[mask], mask) for mask in range(1, QUAD)]
    ring, tail = small_call(join_kv, [ring_of, tail_of], [SMEM] + [VMEM] * QUAD, [meta, *parts])
    row_block = ((2 * tok + TERM_ROWS, wide), BF16)
    packed = small_call(
        pack_rows, [row_block] * QUAD, [SMEM] + [VMEM] * 4 + [ANY],
        [meta, queries, out_grad, attn_out, log_norm, pieces[0]],
        scratch=[pltpu.VMEM((log_norm.shape[2], tok), F32)], cost=4 * 2**20,
    )
    rows = [packed[0]] + [crossed(later(packed[mask], [tail]), mask) for mask in range(1, QUAD)]

    keys = [[ring, shifted(tail, "blk", QUAD)]]
    accs = [None, None]
    sums = [None] * n_z

    def pass_keys(after):
        ring, tail = held(shifted(keys[-1][0], "head", 1), after)
        keys.append([ring, shifted(tail, "blk", QUAD)])

    def keys_and_back(tail, grads):
        pair = ((4, *tail_of[0][1:]), BF16)
        if n_blk != 2 * QUAD:
            tail, grads = shifted(tail, "blk", QUAD), shifted(grads, "blk", -QUAD)
        both = small_call(side_by_side, [pair], [VMEM] * 2, [tail, grads])[0]
        return shifted(both, "blk", QUAD) if n_blk == 2 * QUAD else both

    def call(pair, lag, after=(), parts=1, carried=None):
        heads, grads = attend_call(
            lag, (2 * pair, 2 * pair + 1), n_blk, n_z, meta, block_layout, rows[2 * pair:2 * pair + 2], keys[lag],
            accs[pair], sums[lag], after, parts, carried,
        )
        accs[pair] = heads if lag == n_z - 1 else heads[0]
        sums[lag] = grads[0]
        return grads[-1]

    def send_back(grads):
        return shifted(grads, "blk", -QUAD)

    def pass_sums(lag, back, after):
        out = small_call(pack_sum, [ring_of], [VMEM] * 2 + [ANY], [sums[lag], back, after])[0]
        return out, shifted(out, "head", n_z - 1 - lag)

    call(0, 0)
    pass_keys([accs[0]])
    call(0, 1)
    pass_keys([accs[0]])
    call(0, 2)
    ring, tail = held(shifted(keys[-1][0], "head", 1), [accs[0]])
    back_zero = keys_and_back(tail, call(1, 0, [accs[0]]))
    keys.append([ring, back_zero])
    back_one = send_back(call(1, 1))
    back_two = send_back(call(1, 2))
    call(1, 3)
    out_one, packet_one = pass_sums(1, back_one, accs[1][0])
    cross = ((tok, wide + 2 * HD), BF16)
    whole = pltpu.VMEM(ring_of[0], F32)
    sent = small_call(
        functools.partial(pack_cross, (2, 3)), [cross] * 2, [SMEM] + [VMEM] * 4,
        [meta, *accs[1], sums[0], back_zero], scratch=[whole], cost=2**20,
    )
    out_two, packet_two = pass_sums(2, back_two, out_one)
    back_three = send_back(call(0, 3, [accs[1][0], sent[0], out_two]))
    near_half = ((tok, (wide + 2 * HD) // 2), BF16)
    near_one, near_two, kept = small_call(
        pack_near, [near_half] * 2 + [(piece[0], F32)], [SMEM] + [VMEM] * 3 + [ANY] * 2,
        [meta, accs[0][1], sums[0], back_zero, packet_one, packet_two], scratch=[whole], cost=2**20,
    )
    near_one, near_two = crossed(near_one, 1), crossed(near_two, 1)
    got = [crossed(part, mask) for mask, part in enumerate(sent, 2)]
    hops = small_call(
        split_sum, [piece] * QUAD, [SMEM] + [VMEM] * 4, [meta, sums[3], back_three, packet_one, packet_two],
        scratch=[pltpu.VMEM(ring_of[0], F32)],
    )
    hops = [hopped(hops[mask], mask) for mask in range(QUAD)]
    query_grad, placed = small_call(
        place_heads, [(queries.shape, BF16), ((8, HD), F32)], [SMEM] + [VMEM] * 5, [meta, accs[0][0], near_one, near_two, *got],
        scratch=[pltpu.SemaphoreType.DMA((5,))], far_out=True,
    )
    flat = (key_rows.shape, BF16)
    key_grad, value_grad = small_call(
        finish, [flat, flat], [SMEM] + [VMEM] * 8 + [ANY], [meta, kept, near_two, *got, *hops, placed]
    )
    return query_grad, key_grad, value_grad


def solution(mesh):
    spread = P("blk", "head", None)
    return jax.shard_map(
        shards,
        mesh=mesh,
        in_specs=(spread,) * 6 + (P(),),
        out_specs=(spread,) * 3,
        check_vma=False,
    )
```

```python
import functools
import math

import jax
import jax.numpy as jnp
from jax import lax
from jax.experimental import pallas as pl
from jax.experimental.pallas import tpu as pltpu
from jax.sharding import PartitionSpec as P

HD = 128
GROUP = 8
QUAD = 4
SCALE = 1.0 / math.sqrt(HD)
LOG2E = math.log2(math.e)
FAR = 1e30
TERM_ROWS = 16
COVER = 12
F32 = jnp.float32
BF16 = jnp.bfloat16
SMEM = pl.BlockSpec(memory_space=pltpu.SMEM)
VMEM = pl.BlockSpec(memory_space=pltpu.VMEM)
ANY = pl.BlockSpec(memory_space=pl.ANY)


def shifted(block, axis, distance):
    size = lax.axis_size(axis)
    route = [((i - distance) % size, i) for i in range(size)]
    return lax.ppermute(block, axis, route)


def crossed(block, mask):
    return lax.ppermute(block, "blk", [(i, i ^ mask) for i in range(lax.axis_size("blk"))])


def hopped(block, mask):
    n_z, n_blk = lax.axis_size("head"), lax.axis_size("blk")
    route = [(i * n_blk + b, (i + 1) % n_z * n_blk + (b ^ mask)) for i in range(n_z) for b in range(n_blk)]
    return lax.ppermute(block, ("head", "blk"), route)


def member(meta, mask):
    c = meta[0] % QUAD
    if mask & 1:
        c = c + 1 - 2 * (c % 2)
    if mask & 2:
        c = (c + 2) % QUAD
    return c


def block_of(meta, mask, size):
    return pl.ds(pl.multiple_of(member(meta, mask) * size, size), size)


def pack_kv(meta, keys, vals, *outs):
    for mask, out in enumerate(outs):
        cols = block_of(meta, mask, HD)
        out[0], out[1] = keys[0, :, cols], vals[0, :, cols]


def join_kv(meta, *refs):
    parts, (ring, tail) = refs[:QUAD], refs[QUAD:]
    tok = parts[0].shape[1]
    for mask, part in enumerate(parts):
        ring[:, block_of(meta, mask, tok), :] = part[...]
    tail[...] = ring[:, tok:, :]


def pack_rows(meta, queries, douts, outs, lse, _, *refs):
    packed, lse_t = refs[:QUAD], refs[QUAD]
    tok = queries.shape[1]
    wide = GROUP * HD
    lse_t[...] = lse[0].T * LOG2E
    for mask, out in enumerate(packed):
        cols = block_of(meta, mask, wide)
        out[0:tok, :] = queries[0, :, cols]
        out[tok:2 * tok, :] = douts[0, :, cols]
        norms = lse_t[block_of(meta, mask, GROUP), :]
        for h in range(GROUP):
            at = slice(h * HD, (h + 1) * HD)
            head = pl.ds(pl.multiple_of(member(meta, mask) * wide + h * HD, HD), HD)
            prod = out[tok:2 * tok, at].astype(F32) * outs[0, :, head].astype(F32)
            delta = jnp.sum(prod.T, axis=0, keepdims=True)
            lines = []
            for term in (norms[h:h + 1], delta):
                high = term.astype(BF16).astype(F32)
                lines += [high, term - high]
            block = jnp.concatenate(lines + [jnp.zeros((TERM_ROWS - 4, tok), F32)], axis=0).astype(BF16)
            out[2 * tok:, h * tok:(h + 1) * tok] = block


def do_nothing(*refs):
    del refs


def later(block, after=(), cost=0):
    return pl.pallas_call(
        do_nothing,
        out_shape=jax.ShapeDtypeStruct(block.shape, block.dtype),
        in_specs=[ANY] * (1 + len(after)),
        out_specs=ANY,
        input_output_aliases={0: 0},
        compiler_params=pltpu.CompilerParams(vmem_limit_bytes=2**20),
        cost_estimate=pl.CostEstimate(flops=cost, bytes_accessed=0, transcendentals=0),
        name="later",
    )(block, *after)


def pass_on(ring_in, *refs):
    tail = refs[-1]
    tail[...] = ring_in[:, ring_in.shape[1] - tail.shape[1]:, :]


def held(ring, after):
    planes, rows, cols = ring.shape
    return pl.pallas_call(
        pass_on,
        out_shape=[
            jax.ShapeDtypeStruct(ring.shape, ring.dtype),
            jax.ShapeDtypeStruct((planes, rows // QUAD * (QUAD - 1), cols), ring.dtype),
        ],
        in_specs=[VMEM] + [ANY] * len(after),
        out_specs=[ANY, VMEM],
        input_output_aliases={0: 0},
        compiler_params=pltpu.CompilerParams(vmem_limit_bytes=4 * 2**20),
        name="pass_on",
    )(ring, *after)


def side_by_side(first, second, out):
    out[0:2] = first[...]
    out[2:4] = second[...]


def total(part, n_packet, d_own, back, refs):
    tok = d_own.shape[1] // QUAD
    tail = d_own[:, tok:, :] + back[2 * part:2 * part + 2].astype(F32)
    lead = d_own[:, 0:tok, :]
    if n_packet:
        lead += refs[0][:, 0:tok, :].astype(F32)
        tail += refs[0][:, tok:, :].astype(F32)
    return lead, tail


def pack_sum(part, n_packet, d_own, back, *refs):
    lead, tail = total(part, n_packet, d_own, back, refs)
    out = refs[-1]
    tok = lead.shape[1]
    out[:, 0:tok, :] = lead.astype(BF16)
    out[:, tok:, :] = tail.astype(BF16)


def split_sum(meta, d_own, back, packet, *refs):
    outs, whole = refs[:QUAD], refs[QUAD]
    lead, tail = total(0, 1, d_own, back, (packet,))
    tok = lead.shape[1]
    whole[:, 0:tok, :] = lead
    whole[:, tok:, :] = tail
    for mask, out in enumerate(outs):
        out[...] = whole[:, block_of(meta, mask, tok), :].astype(BF16)


def pack_cross(masks, meta, *refs):
    n = len(masks)
    dqs, (d_own, back), outs, whole = refs[:n], refs[n:n + 2], refs[n + 2:-1], refs[-1]
    lead, tail = total(1, 0, d_own, back, ())
    tok, wide = dqs[0].shape
    whole[:, 0:tok, :] = lead
    whole[:, tok:, :] = tail
    for mask, dq, out in zip(masks, dqs, outs):
        out[:, 0:wide] = dq[...]
        part = whole[:, block_of(meta, mask, tok), :].astype(BF16)
        out[:, wide:wide + HD] = part[0]
        out[:, wide + HD:] = part[1]


def pack_near(meta, dq, d_own, back, first, second, kept, whole):
    lead, tail = total(1, 0, d_own, back, ())
    tok, wide = dq.shape
    half = first.shape[1]
    whole[:, 0:tok, :] = lead
    whole[:, tok:, :] = tail
    part = whole[:, block_of(meta, 1, tok), :].astype(BF16)
    first[...] = dq[:, 0:half]
    second[:, 0:wide - half] = dq[:, half:]
    second[:, wide - half:wide - half + HD] = part[0]
    second[:, wide - half + HD:] = part[1]
    kept[...] = whole[:, block_of(meta, 0, tok), :]


def place_heads(meta, dq_own, near_one, near_two, got_two, got_three, out, done, sems):
    wide = dq_own.shape[1]
    half = near_one.shape[1]
    copies = []
    for mask, src in ((0, dq_own), (2, got_two.at[:, 0:wide]), (3, got_three.at[:, 0:wide])):
        copies.append(pltpu.make_async_copy(src, out.at[0, :, block_of(meta, mask, wide)], sems.at[len(copies)]))
    for start, src in ((0, near_one), (half, near_two.at[:, 0:wide - half])):
        cols = pl.ds(pl.multiple_of(member(meta, 1) * wide + start, HD), src.shape[1])
        copies.append(pltpu.make_async_copy(src, out.at[0, :, cols], sems.at[len(copies)]))
    for copy in copies:
        copy.start()
    done[...] = jnp.zeros_like(done)
    for copy in copies:
        copy.wait()


def finish(meta, kept, near_two, got_two, got_three, hop0, hop1, hop2, hop3, _, dkey, dval):
    for mask, (got, hop) in enumerate(zip((kept, near_two, got_two, got_three), (hop0, hop1, hop2, hop3))):
        cols = block_of(meta, mask, HD)
        for plane, dst in ((0, dkey), (1, dval)):
            if mask == 0:
                first = got[plane]
            else:
                start = got.shape[1] - (2 - plane) * HD
                first = got[:, start:start + HD].astype(F32)
            dst[0, :, cols] = (first + hop[plane].astype(F32)).astype(BF16)


def small_call(body, outs, specs, operands, scratch=(), cost=0, far_out=False):
    shapes = [jax.ShapeDtypeStruct(shape, kind) for shape, kind in outs]
    name = getattr(body, "func", body).__name__
    return pl.pallas_call(
        body,
        out_shape=shapes,
        in_specs=specs,
        out_specs=[ANY if i == 0 and far_out else VMEM for i in range(len(shapes))],
        scratch_shapes=list(scratch),
        compiler_params=pltpu.CompilerParams(vmem_limit_bytes=4 * 2**20),
        cost_estimate=pl.CostEstimate(flops=0, bytes_accessed=cost, transcendentals=0),
        name=name,
    )(*operands)


def attend(lag, masks, n_blk, n_z, first, last, closing, n_after, place, meta, layout, *refs):
    (rows_a, rows_b, near, far), refs = refs[:4], refs[4:]
    tok = near.shape[1] // QUAD
    if not first:
        acc_in, refs = refs[0], refs[1:]
    if closing:
        d_in, refs = refs[0], refs[1:]
    refs = refs[n_after:]
    if last:
        dq_outs, refs = refs[:2], refs[2:]
    else:
        acc_out, refs = refs[0], refs[1:]
    if closing:
        (d_own, d_far), refs = refs[:2], refs[2:]
    else:
        d_out, refs = refs[0], refs[1:]
    kbuf, vbuf, kbuf_t, dbuf, probs, dscores = refs
    n_far = QUAD - 1
    window = QUAD * tok
    quad = meta[0] - meta[0] % QUAD
    z = meta[1]
    shard = (z + n_z - lag) % n_z

    for plane, dst in ((0, kbuf), (1, vbuf)):
        dst[0:n_far * tok, :] = far[plane]
        dst[n_far * tok:, :] = near[plane]
    kbuf_t[...] = kbuf[...].T
    dbuf[...] = d_in[...] if closing else jnp.zeros_like(dbuf)

    def base(group, shard):
        return layout[2 * group + shard // 2] * (2 * tok) + (shard % 2) * tok

    sets = []
    for mask, rows in zip(masks, (rows_a, rows_b)):
        i = member(meta, mask)
        chunk = pl.ds(pl.multiple_of(i * tok, tok), window)
        qbase = base(quad + i, z)
        gaps = [qbase - base((quad + i - n_far + c + n_blk) % n_blk, shard) for c in range(QUAD)]
        sets.append((rows, chunk, gaps))
    row = lax.broadcasted_iota(jnp.int32, (tok, 2 * tok), 0)
    col = lax.broadcasted_iota(jnp.int32, (tok, 2 * tok), 1) % tok
    nt = (((1,), (1,)), ((), ()))
    half = GROUP // 2
    steps = [(t, part) for t in range(2) for part in range(2)]
    scores = {}

    def stacked(rows, start, heads):
        return jnp.concatenate([rows[start:start + tok, h * HD:(h + 1) * HD] for h in heads], axis=0)

    def score_part(t, part):
        rows, chunk, _ = sets[t]
        keys, vals = kbuf[chunk, :], vbuf[chunk, :]
        for g in range(part * half, (part + 1) * half, 2):
            query, dout = stacked(rows, 0, (g, g + 1)), stacked(rows, tok, (g, g + 1))
            scores[t, g] = (
                lax.dot_general(keys, query, nt, preferred_element_type=F32),
                lax.dot_general(vals, dout, nt, preferred_element_type=F32),
            )

    def prob_part(t, part):
        rows, _, gaps = sets[t]
        linked = (col - row + gaps[QUAD - 1]) >= 0
        for g in range(part * half, (part + 1) * half, 2):
            score, dprob = scores.pop((t, g))
            span = slice(g * tok, (g + 2) * tok)
            terms = rows[2 * tok:, span].astype(F32)
            lse, delta = terms[0:1] + terms[1:2], terms[2:3] + terms[3:4]
            for c in range(QUAD):
                at = slice(c * tok, (c + 1) * tok)
                scaled = score[at] * (SCALE * LOG2E)
                if c == QUAD - 1:
                    prob = jnp.where(linked, jnp.exp2(scaled - lse), 0.0)
                else:
                    prob = jnp.exp2(scaled - jnp.where(gaps[c] > 0, lse, FAR))
                probs[t, at, span] = prob.astype(BF16)
                dscores[t, at, span] = (prob * (dprob[at] - delta)).astype(BF16)

    def grad_part(t, part):
        rows, chunk, _ = sets[t]
        heads = range(part * half, (part + 1) * half)
        query, dout = stacked(rows, 0, heads), stacked(rows, tok, heads)
        span = slice(part * half * tok, (part + 1) * half * tok)
        dbuf[0, chunk, :] += jnp.dot(dscores[t, :, span], query, preferred_element_type=F32)
        dbuf[1, chunk, :] += jnp.dot(probs[t, :, span], dout, preferred_element_type=F32)
        dq = jnp.dot(kbuf_t[:, chunk], dscores[t, :, span], preferred_element_type=F32)
        if not first:
            dq = dq + acc_in[t, :, span]
        if last:
            for n, h in enumerate(heads):
                at = slice(h * HD, (h + 1) * HD)
                dq_outs[t][:, at] = (dq[:, n * tok:(n + 1) * tok] * SCALE).T.astype(BF16)
        else:
            acc_out[t, :, span] = dq

    for n in range(len(steps) + 2):
        if n < len(steps):
            score_part(*steps[n])
        if 1 <= n <= len(steps):
            prob_part(*steps[n - 1])
        if n >= 2:
            grad_part(*steps[n - 2])

    if closing:
        for plane, scale in ((0, SCALE), (1, 1.0)):
            d_far[2 * place + plane] = (dbuf[plane, 0:n_far * tok, :] * scale).astype(BF16)
            d_own[plane] = dbuf[plane, n_far * tok:, :] * scale
    else:
        d_out[...] = dbuf[...]


def attend_call(lag, masks, n_blk, n_z, meta, layout, rows, keys, acc, d_in, after, parts, carried):
    tok = keys[0].shape[1] // QUAD
    first, last, closing = acc is None, lag == n_z - 1, d_in is not None
    chunks = (2 * QUAD - 1) * tok
    near, far = (2, QUAD * tok, HD), (2 * parts, (QUAD - 1) * tok, HD)
    outs = (
        [jax.ShapeDtypeStruct((tok, GROUP * HD), BF16)] * 2
        if last else [jax.ShapeDtypeStruct((2, HD, GROUP * tok), F32)]
    )
    n_heads = len(outs)
    if closing:
        outs = outs + [jax.ShapeDtypeStruct(near, F32), jax.ShapeDtypeStruct(far, BF16)]
    else:
        outs = outs + [jax.ShapeDtypeStruct((2, chunks, HD), F32)]
    inputs = [meta, layout, *rows, *keys]
    aliases = {}
    if not first:
        if not last:
            aliases[len(inputs)] = 0
        inputs.append(acc)
    if closing:
        inputs.append(d_in)
    if carried is not None:
        aliases[len(inputs)] = len(outs) - 1
        after = [carried, *after]
    results = pl.pallas_call(
        functools.partial(
            attend, lag, masks, n_blk, n_z, first, last, closing, len(after), int(carried is not None)
        ),
        out_shape=outs,
        in_specs=[SMEM, SMEM] + [VMEM] * (len(inputs) - 2) + [ANY] * len(after),
        out_specs=[VMEM] * len(outs),
        scratch_shapes=[
            pltpu.VMEM((chunks, HD), BF16),
            pltpu.VMEM((chunks, HD), BF16),
            pltpu.VMEM((HD, chunks), BF16),
            pltpu.VMEM((2, chunks, HD), F32),
            pltpu.VMEM((2, QUAD * tok, GROUP * tok), BF16),
            pltpu.VMEM((2, QUAD * tok, GROUP * tok), BF16),
        ],
        input_output_aliases=aliases,
        compiler_params=pltpu.CompilerParams(vmem_limit_bytes=18 * 2**20),
        cost_estimate=pl.CostEstimate(
            flops=COVER * 4 * tok * GROUP * tok * HD, bytes_accessed=2**20, transcendentals=0
        ),
        name="attend",
    )(*inputs, *after)
    return results[:n_heads], results[n_heads:]


def shards(queries, key_rows, value_rows, attn_out, out_grad, log_norm, block_layout):
    tok = queries.shape[1]
    blk, z = lax.axis_index("blk"), lax.axis_index("head")
    n_blk, n_z = lax.axis_size("blk"), lax.axis_size("head")
    wide = GROUP * HD
    meta = jnp.stack([blk, z]).astype(jnp.int32)
    piece = ((2, tok, HD), BF16)
    ring_of, tail_of = ((2, QUAD * tok, HD), BF16), ((2, (QUAD - 1) * tok, HD), BF16)

    pieces = small_call(pack_kv, [piece] * QUAD, [SMEM, VMEM, VMEM], [meta, key_rows, value_rows])
    parts = [pieces[0]] + [crossed(pieces[mask], mask) for mask in range(1, QUAD)]
    ring, tail = small_call(join_kv, [ring_of, tail_of], [SMEM] + [VMEM] * QUAD, [meta, *parts])
    row_block = ((2 * tok + TERM_ROWS, wide), BF16)
    packed = small_call(
        pack_rows, [row_block] * QUAD, [SMEM] + [VMEM] * 4 + [ANY],
        [meta, queries, out_grad, attn_out, log_norm, pieces[0]],
        scratch=[pltpu.VMEM((log_norm.shape[2], tok), F32)], cost=4 * 2**20,
    )
    rows = [packed[0]] + [crossed(later(packed[mask], [tail]), mask) for mask in range(1, QUAD)]

    keys = [[ring, shifted(tail, "blk", QUAD)]]
    accs = [None, None]
    sums = [None] * n_z

    def pass_keys(after):
        ring, tail = held(shifted(keys[-1][0], "head", 1), after)
        keys.append([ring, shifted(tail, "blk", QUAD)])

    def keys_and_back(tail, grads):
        pair = ((4, *tail_of[0][1:]), BF16)
        if n_blk != 2 * QUAD:
            tail, grads = shifted(tail, "blk", QUAD), shifted(grads, "blk", -QUAD)
        both = small_call(side_by_side, [pair], [VMEM] * 2, [tail, grads])[0]
        return shifted(both, "blk", QUAD) if n_blk == 2 * QUAD else both

    def call(pair, lag, after=(), parts=1, carried=None):
        heads, grads = attend_call(
            lag, (2 * pair, 2 * pair + 1), n_blk, n_z, meta, block_layout, rows[2 * pair:2 * pair + 2], keys[lag],
            accs[pair], sums[lag], after, parts, carried,
        )
        accs[pair] = heads if lag == n_z - 1 else heads[0]
        sums[lag] = grads[0]
        return grads[-1]

    def send_back(grads):
        return shifted(grads, "blk", -QUAD)

    def pass_sums(lag, part, back, packet, after):
        parts = [sums[lag], back, *packet]
        out = small_call(
            functools.partial(pack_sum, part, len(packet)), [ring_of], [VMEM] * len(parts) + [ANY], parts + [after]
        )[0]
        return out, [shifted(out, "head", 1)]

    call(0, 0)
    pass_keys([accs[0]])
    call(0, 1)
    pass_keys([accs[0]])
    call(0, 2)
    ring, tail = held(shifted(keys[-1][0], "head", 1), [accs[0]])
    back_zero = keys_and_back(tail, call(1, 0, [accs[0]]))
    keys.append([ring, back_zero])
    back_one = send_back(call(1, 1))
    back_two = send_back(call(1, 2))
    call(1, 3)
    _, packet = pass_sums(1, 0, back_one, [], accs[1][0])
    cross = ((tok, wide + 2 * HD), BF16)
    whole = pltpu.VMEM(ring_of[0], F32)
    sent = small_call(
        functools.partial(pack_cross, (2, 3)), [cross] * 2, [SMEM] + [VMEM] * 4,
        [meta, *accs[1], sums[0], back_zero], scratch=[whole], cost=2**20,
    )
    back_three = send_back(call(0, 3, [accs[1][0], sent[0]]))
    _, packet = pass_sums(2, 0, back_two, packet, sums[3])
    near_half = ((tok, (wide + 2 * HD) // 2), BF16)
    near_one, near_two, kept = small_call(
        pack_near, [near_half] * 2 + [(piece[0], F32)], [SMEM] + [VMEM] * 3,
        [meta, accs[0][1], sums[0], back_zero], scratch=[whole], cost=2**20,
    )
    near_one, near_two = crossed(near_one, 1), crossed(near_two, 1)
    got = [crossed(part, mask) for mask, part in enumerate(sent, 2)]
    hops = small_call(
        split_sum, [piece] * QUAD, [SMEM] + [VMEM] * 3, [meta, sums[3], back_three, *packet],
        scratch=[pltpu.VMEM(ring_of[0], F32)],
    )
    hops = [hopped(hops[mask], mask) for mask in range(QUAD)]
    query_grad, placed = small_call(
        place_heads, [(queries.shape, BF16), ((8, HD), F32)], [SMEM] + [VMEM] * 5, [meta, accs[0][0], near_one, near_two, *got],
        scratch=[pltpu.SemaphoreType.DMA((5,))], far_out=True,
    )
    flat = (key_rows.shape, BF16)
    key_grad, value_grad = small_call(
        finish, [flat, flat], [SMEM] + [VMEM] * 8 + [ANY], [meta, kept, near_two, *got, *hops, placed]
    )
    return query_grad, key_grad, value_grad


def solution(mesh):
    spread = P("blk", "head", None)
    return jax.shard_map(
        shards,
        mesh=mesh,
        in_specs=(spread,) * 6 + (P(),),
        out_specs=(spread,) * 3,
        check_vma=False,
    )
```

```python
import functools
import math

import jax
import jax.numpy as jnp
from jax import lax
from jax.experimental import pallas as pl
from jax.experimental.pallas import tpu as pltpu
from jax.sharding import PartitionSpec as P

HD = 128
GROUP = 8
QUAD = 4
SCALE = 1.0 / math.sqrt(HD)
LOG2E = math.log2(math.e)
FAR = 1e30
TERM_ROWS = 16
COVER = 12
F32 = jnp.float32
BF16 = jnp.bfloat16
SMEM = pl.BlockSpec(memory_space=pltpu.SMEM)
VMEM = pl.BlockSpec(memory_space=pltpu.VMEM)
ANY = pl.BlockSpec(memory_space=pl.ANY)


def shifted(block, axis, distance):
    size = lax.axis_size(axis)
    route = [((i - distance) % size, i) for i in range(size)]
    return lax.ppermute(block, axis, route)


def crossed(block, mask):
    return lax.ppermute(block, "blk", [(i, i ^ mask) for i in range(lax.axis_size("blk"))])


def hopped(block, mask):
    n_z, n_blk = lax.axis_size("head"), lax.axis_size("blk")
    route = [(i * n_blk + b, (i + 1) % n_z * n_blk + (b ^ mask)) for i in range(n_z) for b in range(n_blk)]
    return lax.ppermute(block, ("head", "blk"), route)


def member(meta, mask):
    c = meta[0] % QUAD
    if mask & 1:
        c = c + 1 - 2 * (c % 2)
    if mask & 2:
        c = (c + 2) % QUAD
    return c


def block_of(meta, mask, size):
    return pl.ds(pl.multiple_of(member(meta, mask) * size, size), size)


def pack_kv(meta, keys, vals, *outs):
    for mask, out in enumerate(outs):
        cols = block_of(meta, mask, HD)
        out[0], out[1] = keys[0, :, cols], vals[0, :, cols]


def join_kv(meta, *refs):
    parts, (ring, tail) = refs[:QUAD], refs[QUAD:]
    tok = parts[0].shape[1]
    for mask, part in enumerate(parts):
        ring[:, block_of(meta, mask, tok), :] = part[...]
    tail[...] = ring[:, tok:, :]


def pack_rows(meta, queries, douts, outs, lse, _, *refs):
    packed, lse_t = refs[:QUAD], refs[QUAD]
    tok = queries.shape[1]
    wide = GROUP * HD
    lse_t[...] = lse[0].T * LOG2E
    for mask, out in enumerate(packed):
        cols = block_of(meta, mask, wide)
        out[0:tok, :] = queries[0, :, cols]
        out[tok:2 * tok, :] = douts[0, :, cols]
        norms = lse_t[block_of(meta, mask, GROUP), :]
        for h in range(GROUP):
            at = slice(h * HD, (h + 1) * HD)
            head = pl.ds(pl.multiple_of(member(meta, mask) * wide + h * HD, HD), HD)
            prod = out[tok:2 * tok, at].astype(F32) * outs[0, :, head].astype(F32)
            delta = jnp.sum(prod.T, axis=0, keepdims=True)
            lines = []
            for term in (norms[h:h + 1], delta):
                high = term.astype(BF16).astype(F32)
                lines += [high, term - high]
            block = jnp.concatenate(lines + [jnp.zeros((TERM_ROWS - 4, tok), F32)], axis=0).astype(BF16)
            out[2 * tok:, h * tok:(h + 1) * tok] = block


def do_nothing(*refs):
    del refs


def later(block, after=(), cost=0):
    return pl.pallas_call(
        do_nothing,
        out_shape=jax.ShapeDtypeStruct(block.shape, block.dtype),
        in_specs=[ANY] * (1 + len(after)),
        out_specs=ANY,
        input_output_aliases={0: 0},
        compiler_params=pltpu.CompilerParams(vmem_limit_bytes=2**20),
        cost_estimate=pl.CostEstimate(flops=cost, bytes_accessed=0, transcendentals=0),
        name="later",
    )(block, *after)


def pass_on(ring_in, *refs):
    tail = refs[-1]
    tail[...] = ring_in[:, ring_in.shape[1] - tail.shape[1]:, :]


def held(ring, after):
    planes, rows, cols = ring.shape
    return pl.pallas_call(
        pass_on,
        out_shape=[
            jax.ShapeDtypeStruct(ring.shape, ring.dtype),
            jax.ShapeDtypeStruct((planes, rows // QUAD * (QUAD - 1), cols), ring.dtype),
        ],
        in_specs=[VMEM] + [ANY] * len(after),
        out_specs=[ANY, VMEM],
        input_output_aliases={0: 0},
        compiler_params=pltpu.CompilerParams(vmem_limit_bytes=4 * 2**20),
        name="pass_on",
    )(ring, *after)


def side_by_side(first, second, out):
    out[0:2] = first[...]
    out[2:4] = second[...]


def total(part, n_packet, d_own, back, refs):
    tok = d_own.shape[1] // QUAD
    tail = d_own[:, tok:, :] + back[2 * part:2 * part + 2].astype(F32)
    lead = d_own[:, 0:tok, :]
    if n_packet:
        lead += refs[0][:, 0:tok, :].astype(F32)
        tail += refs[0][:, tok:, :].astype(F32)
    return lead, tail


def pack_sum(part, n_packet, d_own, back, *refs):
    lead, tail = total(part, n_packet, d_own, back, refs)
    out = refs[-1]
    tok = lead.shape[1]
    out[:, 0:tok, :] = lead.astype(BF16)
    out[:, tok:, :] = tail.astype(BF16)


def split_sum(meta, d_own, back, packet, *refs):
    outs, whole = refs[:QUAD], refs[QUAD]
    lead, tail = total(0, 1, d_own, back, (packet,))
    tok = lead.shape[1]
    whole[:, 0:tok, :] = lead
    whole[:, tok:, :] = tail
    for mask, out in enumerate(outs):
        out[...] = whole[:, block_of(meta, mask, tok), :].astype(BF16)


def pack_cross(masks, meta, *refs):
    n = len(masks)
    dqs, (d_own, back), outs, whole = refs[:n], refs[n:n + 2], refs[n + 2:-1], refs[-1]
    lead, tail = total(1, 0, d_own, back, ())
    tok, wide = dqs[0].shape
    whole[:, 0:tok, :] = lead
    whole[:, tok:, :] = tail
    for mask, dq, out in zip(masks, dqs, outs):
        out[:, 0:wide] = dq[...]
        part = whole[:, block_of(meta, mask, tok), :].astype(BF16)
        out[:, wide:wide + HD] = part[0]
        out[:, wide + HD:] = part[1]


def pack_near(meta, dq, d_own, back, first, second, kept, whole):
    lead, tail = total(1, 0, d_own, back, ())
    tok, wide = dq.shape
    half = first.shape[1]
    whole[:, 0:tok, :] = lead
    whole[:, tok:, :] = tail
    part = whole[:, block_of(meta, 1, tok), :].astype(BF16)
    first[...] = dq[:, 0:half]
    second[:, 0:wide - half] = dq[:, half:]
    second[:, wide - half:wide - half + HD] = part[0]
    second[:, wide - half + HD:] = part[1]
    kept[...] = whole[:, block_of(meta, 0, tok), :]


def place_heads(meta, dq_own, near_one, near_two, got_two, got_three, out, done, sems):
    wide = dq_own.shape[1]
    half = near_one.shape[1]
    copies = []
    for mask, src in ((0, dq_own), (2, got_two.at[:, 0:wide]), (3, got_three.at[:, 0:wide])):
        copies.append(pltpu.make_async_copy(src, out.at[0, :, block_of(meta, mask, wide)], sems.at[len(copies)]))
    for start, src in ((0, near_one), (half, near_two.at[:, 0:wide - half])):
        cols = pl.ds(pl.multiple_of(member(meta, 1) * wide + start, HD), src.shape[1])
        copies.append(pltpu.make_async_copy(src, out.at[0, :, cols], sems.at[len(copies)]))
    for copy in copies:
        copy.start()
    done[...] = jnp.zeros_like(done)
    for copy in copies:
        copy.wait()


def finish(meta, kept, near_two, got_two, got_three, hop0, hop1, hop2, hop3, _, dkey, dval):
    for mask, (got, hop) in enumerate(zip((kept, near_two, got_two, got_three), (hop0, hop1, hop2, hop3))):
        cols = block_of(meta, mask, HD)
        for plane, dst in ((0, dkey), (1, dval)):
            if mask == 0:
                first = got[plane]
            else:
                start = got.shape[1] - (2 - plane) * HD
                first = got[:, start:start + HD].astype(F32)
            dst[0, :, cols] = (first + hop[plane].astype(F32)).astype(BF16)


def small_call(body, outs, specs, operands, scratch=(), cost=0, far_out=False):
    shapes = [jax.ShapeDtypeStruct(shape, kind) for shape, kind in outs]
    name = getattr(body, "func", body).__name__
    return pl.pallas_call(
        body,
        out_shape=shapes,
        in_specs=specs,
        out_specs=[ANY if i == 0 and far_out else VMEM for i in range(len(shapes))],
        scratch_shapes=list(scratch),
        compiler_params=pltpu.CompilerParams(vmem_limit_bytes=4 * 2**20),
        cost_estimate=pl.CostEstimate(flops=0, bytes_accessed=cost, transcendentals=0),
        name=name,
    )(*operands)


def attend(lag, masks, n_blk, n_z, first, last, closing, n_after, place, meta, layout, *refs):
    (rows_a, rows_b, near, far), refs = refs[:4], refs[4:]
    tok = near.shape[1] // QUAD
    if not first:
        acc_in, refs = refs[0], refs[1:]
    if closing:
        d_in, refs = refs[0], refs[1:]
    refs = refs[n_after:]
    if last:
        dq_outs, refs = refs[:2], refs[2:]
    else:
        acc_out, refs = refs[0], refs[1:]
    if closing:
        (d_own, d_far), refs = refs[:2], refs[2:]
    else:
        d_out, refs = refs[0], refs[1:]
    kbuf, vbuf, kbuf_t, dbuf, probs, dscores = refs
    n_far = QUAD - 1
    window = QUAD * tok
    quad = meta[0] - meta[0] % QUAD
    z = meta[1]
    shard = (z + n_z - lag) % n_z

    for plane, dst in ((0, kbuf), (1, vbuf)):
        dst[0:n_far * tok, :] = far[plane]
        dst[n_far * tok:, :] = near[plane]
    kbuf_t[...] = kbuf[...].T
    dbuf[...] = d_in[...] if closing else jnp.zeros_like(dbuf)

    def base(group, shard):
        return layout[2 * group + shard // 2] * (2 * tok) + (shard % 2) * tok

    sets = []
    for mask, rows in zip(masks, (rows_a, rows_b)):
        i = member(meta, mask)
        chunk = pl.ds(pl.multiple_of(i * tok, tok), window)
        qbase = base(quad + i, z)
        gaps = [qbase - base((quad + i - n_far + c + n_blk) % n_blk, shard) for c in range(QUAD)]
        sets.append((rows, chunk, gaps))
    row = lax.broadcasted_iota(jnp.int32, (tok, 2 * tok), 0)
    col = lax.broadcasted_iota(jnp.int32, (tok, 2 * tok), 1) % tok
    nt = (((1,), (1,)), ((), ()))
    half = GROUP // 2
    steps = [(t, part) for t in range(2) for part in range(2)]
    scores = {}

    def stacked(rows, start, heads):
        return jnp.concatenate([rows[start:start + tok, h * HD:(h + 1) * HD] for h in heads], axis=0)

    def score_part(t, part):
        rows, chunk, _ = sets[t]
        keys, vals = kbuf[chunk, :], vbuf[chunk, :]
        for g in range(part * half, (part + 1) * half, 2):
            query, dout = stacked(rows, 0, (g, g + 1)), stacked(rows, tok, (g, g + 1))
            scores[t, g] = (
                lax.dot_general(keys, query, nt, preferred_element_type=F32),
                lax.dot_general(vals, dout, nt, preferred_element_type=F32),
            )

    def prob_part(t, part):
        rows, _, gaps = sets[t]
        linked = (col - row + gaps[QUAD - 1]) >= 0
        for g in range(part * half, (part + 1) * half, 2):
            score, dprob = scores.pop((t, g))
            span = slice(g * tok, (g + 2) * tok)
            terms = rows[2 * tok:, span].astype(F32)
            lse, delta = terms[0:1] + terms[1:2], terms[2:3] + terms[3:4]
            for c in range(QUAD):
                at = slice(c * tok, (c + 1) * tok)
                scaled = score[at] * (SCALE * LOG2E)
                if c == QUAD - 1:
                    prob = jnp.where(linked, jnp.exp2(scaled - lse), 0.0)
                else:
                    prob = jnp.exp2(scaled - jnp.where(gaps[c] > 0, lse, FAR))
                probs[t, at, span] = prob.astype(BF16)
                dscores[t, at, span] = (prob * (dprob[at] - delta)).astype(BF16)

    def grad_part(t, part):
        rows, chunk, _ = sets[t]
        heads = range(part * half, (part + 1) * half)
        query, dout = stacked(rows, 0, heads), stacked(rows, tok, heads)
        span = slice(part * half * tok, (part + 1) * half * tok)
        dbuf[0, chunk, :] += jnp.dot(dscores[t, :, span], query, preferred_element_type=F32)
        dbuf[1, chunk, :] += jnp.dot(probs[t, :, span], dout, preferred_element_type=F32)
        dq = jnp.dot(kbuf_t[:, chunk], dscores[t, :, span], preferred_element_type=F32)
        if not first:
            dq = dq + acc_in[t, :, span]
        if last:
            for n, h in enumerate(heads):
                at = slice(h * HD, (h + 1) * HD)
                dq_outs[t][:, at] = (dq[:, n * tok:(n + 1) * tok] * SCALE).T.astype(BF16)
        else:
            acc_out[t, :, span] = dq

    for n in range(len(steps) + 2):
        if n < len(steps):
            score_part(*steps[n])
        if 1 <= n <= len(steps):
            prob_part(*steps[n - 1])
        if n >= 2:
            grad_part(*steps[n - 2])

    if closing:
        for plane, scale in ((0, SCALE), (1, 1.0)):
            d_far[2 * place + plane] = (dbuf[plane, 0:n_far * tok, :] * scale).astype(BF16)
            d_own[plane] = dbuf[plane, n_far * tok:, :] * scale
    else:
        d_out[...] = dbuf[...]


def attend_call(lag, masks, n_blk, n_z, meta, layout, rows, keys, acc, d_in, after, parts, carried):
    tok = keys[0].shape[1] // QUAD
    first, last, closing = acc is None, lag == n_z - 1, d_in is not None
    chunks = (2 * QUAD - 1) * tok
    near, far = (2, QUAD * tok, HD), (2 * parts, (QUAD - 1) * tok, HD)
    outs = (
        [jax.ShapeDtypeStruct((tok, GROUP * HD), BF16)] * 2
        if last else [jax.ShapeDtypeStruct((2, HD, GROUP * tok), F32)]
    )
    n_heads = len(outs)
    if closing:
        outs = outs + [jax.ShapeDtypeStruct(near, F32), jax.ShapeDtypeStruct(far, BF16)]
    else:
        outs = outs + [jax.ShapeDtypeStruct((2, chunks, HD), F32)]
    inputs = [meta, layout, *rows, *keys]
    aliases = {}
    if not first:
        if not last:
            aliases[len(inputs)] = 0
        inputs.append(acc)
    if closing:
        inputs.append(d_in)
    if carried is not None:
        aliases[len(inputs)] = len(outs) - 1
        after = [carried, *after]
    results = pl.pallas_call(
        functools.partial(
            attend, lag, masks, n_blk, n_z, first, last, closing, len(after), int(carried is not None)
        ),
        out_shape=outs,
        in_specs=[SMEM, SMEM] + [VMEM] * (len(inputs) - 2) + [ANY] * len(after),
        out_specs=[VMEM] * len(outs),
        scratch_shapes=[
            pltpu.VMEM((chunks, HD), BF16),
            pltpu.VMEM((chunks, HD), BF16),
            pltpu.VMEM((HD, chunks), BF16),
            pltpu.VMEM((2, chunks, HD), F32),
            pltpu.VMEM((2, QUAD * tok, GROUP * tok), BF16),
            pltpu.VMEM((2, QUAD * tok, GROUP * tok), BF16),
        ],
        input_output_aliases=aliases,
        compiler_params=pltpu.CompilerParams(vmem_limit_bytes=18 * 2**20),
        cost_estimate=pl.CostEstimate(
            flops=COVER * 4 * tok * GROUP * tok * HD, bytes_accessed=2**20, transcendentals=0
        ),
        name="attend",
    )(*inputs, *after)
    return results[:n_heads], results[n_heads:]


def shards(queries, key_rows, value_rows, attn_out, out_grad, log_norm, block_layout):
    tok = queries.shape[1]
    blk, z = lax.axis_index("blk"), lax.axis_index("head")
    n_blk, n_z = lax.axis_size("blk"), lax.axis_size("head")
    wide = GROUP * HD
    meta = jnp.stack([blk, z]).astype(jnp.int32)
    piece = ((2, tok, HD), BF16)
    ring_of, tail_of = ((2, QUAD * tok, HD), BF16), ((2, (QUAD - 1) * tok, HD), BF16)

    pieces = small_call(pack_kv, [piece] * QUAD, [SMEM, VMEM, VMEM], [meta, key_rows, value_rows])
    parts = [pieces[0]] + [crossed(pieces[mask], mask) for mask in range(1, QUAD)]
    ring, tail = small_call(join_kv, [ring_of, tail_of], [SMEM] + [VMEM] * QUAD, [meta, *parts])
    row_block = ((2 * tok + TERM_ROWS, wide), BF16)
    packed = small_call(
        pack_rows, [row_block] * QUAD, [SMEM] + [VMEM] * 4 + [ANY],
        [meta, queries, out_grad, attn_out, log_norm, pieces[0]],
        scratch=[pltpu.VMEM((log_norm.shape[2], tok), F32)], cost=4 * 2**20,
    )
    rows = [packed[0]] + [crossed(later(packed[mask], [tail]), mask) for mask in range(1, QUAD)]

    keys = [[ring, shifted(tail, "blk", QUAD)]]
    accs = [None, None]
    sums = [None] * n_z

    def pass_keys(after):
        ring, tail = held(shifted(keys[-1][0], "head", 1), after)
        keys.append([ring, shifted(tail, "blk", QUAD)])

    def keys_and_back(tail, grads):
        pair = ((4, *tail_of[0][1:]), BF16)
        if n_blk != 2 * QUAD:
            tail, grads = shifted(tail, "blk", QUAD), shifted(grads, "blk", -QUAD)
        both = small_call(side_by_side, [pair], [VMEM] * 2, [tail, grads])[0]
        return shifted(both, "blk", QUAD) if n_blk == 2 * QUAD else both

    def call(pair, lag, after=(), parts=1, carried=None):
        heads, grads = attend_call(
            lag, (2 * pair, 2 * pair + 1), n_blk, n_z, meta, block_layout, rows[2 * pair:2 * pair + 2], keys[lag],
            accs[pair], sums[lag], after, parts, carried,
        )
        accs[pair] = heads if lag == n_z - 1 else heads[0]
        sums[lag] = grads[0]
        return grads[-1]

    def send_back(grads):
        return shifted(grads, "blk", -QUAD)

    def pass_sums(lag, part, back, packet, after):
        parts = [sums[lag], back, *packet]
        out = small_call(
            functools.partial(pack_sum, part, len(packet)), [ring_of], [VMEM] * len(parts) + [ANY], parts + [after]
        )[0]
        return out, [shifted(out, "head", 1)]

    call(0, 0)
    pass_keys([accs[0]])
    call(0, 1)
    pass_keys([accs[0]])
    call(0, 2)
    ring, tail = held(shifted(keys[-1][0], "head", 1), [accs[0]])
    back_zero = keys_and_back(tail, call(1, 0, [accs[0]]))
    keys.append([ring, back_zero])
    back_one = send_back(call(1, 1))
    back_two = send_back(call(1, 2))
    call(1, 3)
    _, packet = pass_sums(1, 0, back_one, [], accs[1][0])
    cross = ((tok, wide + 2 * HD), BF16)
    whole = pltpu.VMEM(ring_of[0], F32)
    sent = small_call(
        functools.partial(pack_cross, (2, 3)), [cross] * 2, [SMEM] + [VMEM] * 4,
        [meta, *accs[1], sums[0], back_zero], scratch=[whole], cost=2**20,
    )
    back_three = send_back(call(0, 3, [accs[1][0]]))
    _, packet = pass_sums(2, 0, back_two, packet, sums[3])
    near_half = ((tok, (wide + 2 * HD) // 2), BF16)
    near_one, near_two, kept = small_call(
        pack_near, [near_half] * 2 + [(piece[0], F32)], [SMEM] + [VMEM] * 3,
        [meta, accs[0][1], sums[0], back_zero], scratch=[whole], cost=2**20,
    )
    near_one, near_two = crossed(near_one, 1), crossed(near_two, 1)
    got = [crossed(part, mask) for mask, part in enumerate(sent, 2)]
    hops = small_call(
        split_sum, [piece] * QUAD, [SMEM] + [VMEM] * 3, [meta, sums[3], back_three, *packet],
        scratch=[pltpu.VMEM(ring_of[0], F32)],
    )
    hops = [hopped(hops[mask], mask) for mask in range(QUAD)]
    query_grad, placed = small_call(
        place_heads, [(queries.shape, BF16), ((8, HD), F32)], [SMEM] + [VMEM] * 5, [meta, accs[0][0], near_one, near_two, *got],
        scratch=[pltpu.SemaphoreType.DMA((5,))], far_out=True,
    )
    flat = (key_rows.shape, BF16)
    key_grad, value_grad = small_call(
        finish, [flat, flat], [SMEM] + [VMEM] * 8 + [ANY], [meta, kept, near_two, *got, *hops, placed]
    )
    return query_grad, key_grad, value_grad


def solution(mesh):
    spread = P("blk", "head", None)
    return jax.shard_map(
        shards,
        mesh=mesh,
        in_specs=(spread,) * 6 + (P(),),
        out_specs=(spread,) * 3,
        check_vma=False,
    )
```
